32 devices in a mesh: grp: 2 (over y), ctx: 4 (over z), head: 4 (over x, core).
Axes of the slice: x: 2, y: 2, z: 4, core: 2. Of those that a mesh axis runs over, the one named last changes fastest.
Arguments:
- behavior_embed: bfloat16 [4, 2048, 256], P('grp', 'ctx'), parts along dimension 0, may hold values from -6 to 6
- behavior_mask: int32 [4, 2048], P('grp', 'ctx'), parts along dimension 0, may hold values 0 or 1
- history_len: int32 [4], P('grp'), parts along dimension 0, may hold values from 256 to 2048, as said below
- log_decay: float32 [8, 4, 2048], P('head', 'grp', 'ctx'), parts along dimension 1, may hold values from -2 to 0
- candidate_embed: bfloat16 [4, 512, 256], P('grp', 'ctx'), parts along dimension 0, may hold values from -6 to 6
- input_weight: bfloat16 [256, 1024], replicated, may hold values from -0.375 to 0.375
- input_gain: float32 [1024], replicated, may hold values from 0.5 to 1.5
- proj_weight: bfloat16 [4, 1024, 1024], P(None, None, 'head'), may hold values from -0.1875 to 0.1875
- output_gain: float32 [1024], P('head'), may hold values from 0.5 to 1.5
- ranker_first: bfloat16 [1024, 1024], P('head'), may hold values from -0.1875 to 0.1875
- ranker_second: bfloat16 [1024], replicated, may hold values from -0.1875 to 0.1875
Outputs:
- history_out: bfloat16 [4, 2048, 1024], P('grp', 'ctx', 'head'), parts along dimension 0
- scores: float32 [4, 512], P('grp', ('ctx', 'head')), parts along dimension 0
The draws below stay inside these ranges and needn't reach their ends.
There are 2 independent parts, one for each index of `grp`. The reference program is written for one: setup_inputs(seed, part) draws one part's arguments, and reference() takes and returns one part's arrays. A program takes and returns all parts, laid end to end along the dimension named above; an argument that names none is the same for every part. Nothing has to cross between parts.
Inputs may be any that keep to these rules, and one draw needn't show every extreme that they name: Histories are padded at the start: the last history_len[u] positions hold user u's behaviors; at least one user's history fills all 2048 positions.
All inputs are finite; a program needn't handle non-finite values. No bound on the sum of `behavior_mask` on one device may be relied on, other than what follows from the above.
Results may differ from the reference program's by a relative error of at most 0.0098.
Values may be sent and summed in bfloat16 or wider, within the bound.
A program may use at most 64 MiB of HBM per device.

```python
import math
import jax
import jax.numpy as jnp
from jax import lax

USER_GROUP_SIZE = 2
L_DEV = 512
HEAD_TOTAL = 8
DH = 128
D = 1024
E = 256
MLP_H = 1024
BEHAVIOR_LENGTH = 2048
CAND = 512


def draw_log_decay(key, part):
    random_subkeys = jax.random.split(key, 7)
    fast_share = 0.5
    slow_low = math.log(0.1)
    slow_high = math.log(0.4)
    fast_head = jax.random.uniform(random_subkeys[0], (HEAD_TOTAL, 1, 1)) < fast_share
    fast_rate = jnp.exp(jax.random.uniform(random_subkeys[1], (HEAD_TOTAL, 1, 1), minval=-0.3, maxval=0.3)) / 40.0
    slow_rate = jnp.exp(jax.random.uniform(random_subkeys[2], (HEAD_TOTAL, 1, 1), minval=slow_low, maxval=slow_high)) * math.log(10.0) / BEHAVIOR_LENGTH
    per_position_rate = jnp.where(fast_head, fast_rate, slow_rate)
    segment_count = BEHAVIOR_LENGTH // L_DEV
    segment_weight = jnp.exp(jax.random.uniform(random_subkeys[3], (1, USER_GROUP_SIZE, segment_count, 1), minval=-0.7, maxval=0.7))
    segment_weight = jnp.broadcast_to(segment_weight, (1, USER_GROUP_SIZE, segment_count, L_DEV)).reshape(1, USER_GROUP_SIZE, BEHAVIOR_LENGTH)
    position_weight = jnp.exp(jax.random.uniform(random_subkeys[4], (HEAD_TOTAL, USER_GROUP_SIZE, BEHAVIOR_LENGTH), minval=-0.7, maxval=0.7))
    spike_location = jax.random.randint(random_subkeys[5], (HEAD_TOTAL, USER_GROUP_SIZE, 2), 0, BEHAVIOR_LENGTH)
    spike_length = jnp.log(jax.random.uniform(random_subkeys[6], (HEAD_TOTAL, USER_GROUP_SIZE, 2), minval=0.5, maxval=0.8))
    position_indices = jnp.arange(BEHAVIOR_LENGTH, dtype=jnp.int32)
    activity_spikes = jnp.sum(jnp.where(position_indices[None, None, None, :] == spike_location[..., None], spike_length[..., None], 0.0), axis=2)
    return (-per_position_rate * segment_weight * position_weight + activity_spikes).astype(jnp.float32)


def draw_history_len(key, part):
    random_subkeys = jax.random.split(key, 2)
    lengths = jax.random.randint(random_subkeys[0], (USER_GROUP_SIZE,), BEHAVIOR_LENGTH // 8, BEHAVIOR_LENGTH + 1)
    full_user = jax.random.randint(random_subkeys[1], (), 0, USER_GROUP_SIZE)
    return jnp.where(jnp.arange(USER_GROUP_SIZE) == full_user, BEHAVIOR_LENGTH, lengths).astype(jnp.int32)


def set_ends(array, stream_key, least, high):
    spot = [jax.random.randint(jax.random.fold_in(stream_key, axis), (), 0, length) for axis, length in enumerate(array.shape)]
    widest = array.shape.index(max(array.shape))
    beside = spot[:widest] + [(spot[widest] + 1) % array.shape[widest]] + spot[widest + 1:]
    return array.at[tuple(spot)].set(least).at[tuple(beside)].set(high)


def block_levels(stream_key, extent, cuts, low, largest):
    def one(position, blocks):
        draws = jax.random.uniform(jax.random.fold_in(jax.random.fold_in(stream_key, 6), position), (blocks,), jnp.float32, low / len(cuts), largest / len(cuts))
        return jnp.repeat(jnp.exp(draws), extent[position] // blocks).reshape((-1,) + (1,) * (len(extent) - position - 1))

    factor_of = one(*cuts[0])
    for cut in cuts[1:]:
        factor_of = factor_of * one(*cut)
    return factor_of


def bell_draw(stream_key, dims, deviation, most, shards=(), kind=jnp.bfloat16):
    level = block_levels(stream_key, dims, shards, -0.22, 0.18) if shards else 1.0
    values = jax.random.normal(stream_key, dims, jnp.float32) * deviation * level
    return jnp.minimum(jnp.maximum(values, -most), most).astype(kind)


def setup_inputs(seed: int = 0, part: int = 0) -> dict:
    arg_keys = jax.random.split(jax.random.key(seed), 12)
    part_splits = jax.random.split(jax.random.fold_in(arg_keys[11], part), 12)
    return {
        "behavior_embed": bell_draw(part_splits[0], (USER_GROUP_SIZE, BEHAVIOR_LENGTH, E), 1.0, 6.0, ((1, 4),)),
        "behavior_mask": set_ends((jax.random.randint(part_splits[1], (USER_GROUP_SIZE, BEHAVIOR_LENGTH), 0, 8) < 7).astype(jnp.int32), jax.random.fold_in(part_splits[1], 1), 0, 1),
        "history_len": draw_history_len(jax.random.fold_in(jax.random.fold_in(arg_keys[11], part), 71), part),
        "log_decay": draw_log_decay(jax.random.fold_in(jax.random.fold_in(arg_keys[11], part), 71), part),
        "candidate_embed": bell_draw(part_splits[4], (USER_GROUP_SIZE, CAND, E), 1.0, 6.0, ((1, 4),)),
        "input_weight": bell_draw(arg_keys[5], (E, D), E ** -0.5, 0.375),
        "input_gain": jnp.clip(1.0 + 0.1 * jax.random.normal(arg_keys[6], (D,), jnp.float32), 0.5, 1.5),
        "proj_weight": bell_draw(arg_keys[7], (4, D, D), D ** -0.5, 0.1875, ((2, 4),)),
        "output_gain": jnp.clip(1.0 + 0.1 * jax.random.normal(arg_keys[8], (D,), jnp.float32), 0.5, 1.5),
        "ranker_first": bell_draw(arg_keys[9], (D, MLP_H), D ** -0.5, 0.1875, ((0, 4),)),
        "ranker_second": bell_draw(arg_keys[10], (MLP_H,), MLP_H ** -0.5, 0.1875),
    }


epsilon = 1e-05
highest = lax.Precision.HIGHEST

def rms_norm(values, gain_row):
    mean_square = lax.optimization_barrier(jnp.mean(values * values, axis=-1, keepdims=True))
    return values * lax.rsqrt(mean_square + epsilon) * gain_row

def features(embed_rows, input_weight, input_gain):
    embedded = embed_rows.reshape(-1, embed_rows.shape[-1])
    rounded = lax.optimization_barrier(jnp.dot(embedded, input_weight, preferred_element_type=jnp.float32).astype(jnp.bfloat16))
    return rms_norm(rounded.astype(jnp.float32), input_gain).astype(jnp.bfloat16)

def reference(behavior_embed, behavior_mask, history_len, log_decay, candidate_embed, input_weight, input_gain, proj_weight, output_gain, ranker_first, ranker_second):
    position_indices = jnp.arange(BEHAVIOR_LENGTH, dtype=jnp.int32)
    valid_mask = ((position_indices[None, :] >= BEHAVIOR_LENGTH - history_len[:, None]) & (behavior_mask == 1)).astype(jnp.float32)
    behavior_norm = features(behavior_embed, input_weight, input_gain)
    candidate_norm = features(candidate_embed, input_weight, input_gain)
    query_rows = jnp.dot(behavior_norm, proj_weight[0], preferred_element_type=jnp.float32).astype(jnp.bfloat16)
    key_rows = (jnp.dot(behavior_norm, proj_weight[1], preferred_element_type=jnp.float32) * DH ** (-0.5)).astype(jnp.bfloat16)
    value_rows = jnp.dot(behavior_norm, proj_weight[2], preferred_element_type=jnp.float32).astype(jnp.bfloat16)
    gate_rows = jnp.dot(behavior_norm, proj_weight[3], preferred_element_type=jnp.float32).astype(jnp.bfloat16)
    blocks = BEHAVIOR_LENGTH // L_DEV

    def by_block(rows):
        return jnp.transpose(rows.reshape(USER_GROUP_SIZE, blocks, L_DEV, HEAD_TOTAL, DH), (1, 0, 2, 3, 4)).astype(jnp.float32)
    decay_blocks = jnp.transpose(log_decay.reshape(HEAD_TOTAL, USER_GROUP_SIZE, blocks, L_DEV), (2, 0, 1, 3))
    mask_blocks = jnp.transpose(valid_mask.reshape(USER_GROUP_SIZE, blocks, L_DEV), (1, 0, 2))
    row_ids = jnp.arange(L_DEV)
    causal = row_ids[:, None] >= row_ids[None, :]

    def step_block(carry_state, inputs):
        query_block, key_block, value_block, decay_block, mask_block = inputs
        cumulative = jnp.cumsum(decay_block, axis=-1)
        span_total = cumulative[..., -1]
        log_gap = cumulative[..., :, None] - cumulative[..., None, :]
        decay_matrix = jnp.where(causal, jnp.exp(jnp.where(causal, log_gap, 0.0)), 0.0) * mask_block[None, :, None, :]
        scores_local = jnp.einsum('uihd,ujhd->huij', query_block, key_block, precision=highest)
        within = jnp.einsum('huij,ujhd->uihd', scores_local * decay_matrix, value_block, precision=highest)
        carried = jnp.einsum('uihd,hude->uihe', query_block, carry_state, precision=highest) * jnp.exp(jnp.transpose(cumulative, (1, 2, 0)))[..., None]
        key_weight = jnp.exp(span_total[..., None] - cumulative) * mask_block[None]
        local_state = jnp.einsum('ujhd,ujhe->hude', key_block * jnp.transpose(key_weight, (1, 2, 0))[..., None], value_block, precision=highest)
        next_state = jnp.exp(span_total)[..., None, None] * carry_state + local_state
        return (next_state, within + carried)
    initial = jnp.zeros((HEAD_TOTAL, USER_GROUP_SIZE, DH, DH), jnp.float32)
    final_full, readout = lax.scan(step_block, initial, (by_block(query_rows), by_block(key_rows), by_block(value_rows), decay_blocks, mask_blocks))
    readout = jnp.transpose(readout, (1, 0, 2, 3, 4)).reshape(USER_GROUP_SIZE, BEHAVIOR_LENGTH, HEAD_TOTAL, DH)
    gain_heads = output_gain.reshape(HEAD_TOTAL, DH)
    gate_wide = gate_rows.astype(jnp.float32).reshape(USER_GROUP_SIZE, BEHAVIOR_LENGTH, HEAD_TOTAL, DH)
    history_out = (rms_norm(readout, gain_heads) * jax.nn.silu(gate_wide)).reshape(USER_GROUP_SIZE, BEHAVIOR_LENGTH, D).astype(jnp.bfloat16)
    final_state = final_full.astype(jnp.bfloat16)
    candidate_query = jnp.dot(candidate_norm, proj_weight[0], preferred_element_type=jnp.float32).astype(jnp.bfloat16).reshape(USER_GROUP_SIZE, CAND, HEAD_TOTAL, DH)
    candidate_read = jnp.einsum('uchd,hude->uche', candidate_query.astype(jnp.float32), final_state.astype(jnp.float32), precision=highest)
    candidate_feat = (rms_norm(candidate_read, gain_heads).reshape(USER_GROUP_SIZE * CAND, D) + candidate_norm.astype(jnp.float32)).astype(jnp.bfloat16)
    hidden = jnp.dot(candidate_feat, ranker_first, preferred_element_type=jnp.float32)
    scores = jnp.dot(jax.nn.silu(hidden), ranker_second.astype(jnp.float32), precision=highest).reshape(USER_GROUP_SIZE, CAND)
    return (history_out, scores)
```

```python
import functools

import jax
import jax.numpy as jnp
from jax import lax
from jax.experimental import pallas as pl
from jax.experimental.pallas import tpu as pltpu
from jax.sharding import PartitionSpec as P

DH = 128
CORES = 2
EPS = 1e-05
F32 = jnp.float32
BF16 = jnp.bfloat16
MESH = pl.DeviceIdType.MESH


def mm(a, b):
    return jnp.dot(a, b, preferred_element_type=F32)


def mm_tn(a, b):
    return lax.dot_general(a, b, (((0,), (0,)), ((), ())), preferred_element_type=F32)


def mm_nt(a, b):
    return lax.dot_general(a, b, (((1,), (1,)), ((), ())), preferred_element_type=F32)


def silu(x):
    return x / (1.0 + jnp.exp(-x))


def normed(rows, weight, gain):
    raw = mm(rows, weight).astype(BF16).astype(F32)
    scale = lax.rsqrt(jnp.mean(raw * raw, axis=-1, keepdims=True) + EPS)
    return (raw * scale * gain).astype(BF16)


def kernel(
    n_ctx,
    n_head,
    chunk,
    hl,
    be_h,
    mk_h,
    ld_h,
    ce_h,
    iw_h,
    ig_h,
    pw_h,
    og_h,
    rf_h,
    r2_h,
    hist_h,
    score_o,
    be,
    mk,
    ld,
    ce,
    iw,
    ig,
    pw,
    og,
    r2,
    rank,
    norm_s,
    cnorm,
    key_s,
    val_s,
    qry_s,
    gate_s,
    within_s,
    hist,
    dat,
    lst,
    loc,
    tall,
    p_in,
    p_out,
    x_in,
    x_out,
    feat,
    feat_in,
    load_sem,
    out_sem,
    t_send,
    t_recv,
    p_send,
    p_recv,
    x_send,
    x_recv,
    r_send,
    r_recv,
    f_send,
    f_recv,
):
    users, span, _ = be.shape
    cand = ce.shape[1]
    cols = og.shape[1]
    heads = cols // DH
    pairs = heads * users
    chunks = span // chunk
    share = cand // n_head
    me = lax.axis_index("ctx")
    hm = lax.axis_index("head")
    core = lax.rem(hm, CORES)

    loads = {}
    for i, (name, src, dst) in enumerate(
        (
            ("be", be_h, be),
            ("iw", iw_h, iw),
            ("ig", ig_h, ig),
            ("ld", ld_h, ld),
            ("mk", mk_h, mk),
            ("k", pw_h.at[1], pw.at[1]),
            ("v", pw_h.at[2], pw.at[2]),
            ("rf", rf_h, rank.at[hm]),
            ("q", pw_h.at[0], pw.at[0]),
            ("g", pw_h.at[3], pw.at[3]),
            ("og", og_h, og),
            ("ce", ce_h, ce),
            ("r2", r2_h, r2),
        )
    ):
        loads[name] = pltpu.make_async_copy(src, dst, load_sem.at[i])
        loads[name].start()

    barrier = pltpu.get_barrier_semaphore()
    for k in range(1, n_ctx):
        pl.semaphore_signal(
            barrier, inc=1, device_id={"ctx": lax.rem(me + k, n_ctx)}, device_id_type=MESH
        )
    for k in range(1, n_head):
        pl.semaphore_signal(
            barrier, inc=1, device_id={"head": lax.rem(hm + k, n_head)}, device_id_type=MESH
        )

    loads["ld"].wait()
    loads["mk"].wait()
    dat[...] = jnp.zeros_like(dat)
    for h in range(heads):
        dat[h * users : (h + 1) * users, :] = ld[h]
    cum = dat[0:8, :]
    lane = lax.broadcasted_iota(jnp.int32, (8, span), 1)
    in_chunk = lax.rem(lane, chunk)
    step = 1
    while step < chunk:
        cum = cum + jnp.where(in_chunk >= step, pltpu.roll(cum, step, 1), 0.0)
        step *= 2
    ends = [cum[:, (c + 1) * chunk - 1 : (c + 1) * chunk] for c in range(chunks)]
    fades = [jnp.exp(e) for e in ends]
    end_total = functools.reduce(jnp.add, ends)
    fade_total = jnp.exp(end_total)
    end_row = ends[-1]
    for c in range(chunks - 2, -1, -1):
        end_row = jnp.where(lane < (c + 1) * chunk, ends[c], end_row)
    weight_rows = jnp.exp(end_row - cum)
    dat[0:8, :] = cum
    dat[8:16, :] = weight_rows
    dat[16:24, :] = jnp.exp(cum)
    pos = me * span + lax.broadcasted_iota(jnp.int32, (1, span), 1)
    valid = []
    for u in range(users):
        keep = (pos >= n_ctx * span - hl[u]) & (mk[u : u + 1, :] == 1)
        valid.append(jnp.where(keep, 1.0, 0.0))
    for h in range(heads):
        for u in range(users):
            p = 8 + h * users + u
            dat[p : p + 1, :] = dat[p : p + 1, :] * valid[u]
    col = jnp.transpose(dat[...])
    tall[me] = jnp.broadcast_to(end_total, (8, 128))

    pl.semaphore_wait(barrier, n_ctx + n_head - 2)

    t_copies = []
    for k in range(1, n_ctx):
        cp = pltpu.make_async_remote_copy(
            src_ref=tall.at[me],
            dst_ref=tall.at[me],
            send_sem=t_send.at[k],
            recv_sem=t_recv.at[me],
            device_id={"ctx": lax.rem(me + k, n_ctx)},
            device_id_type=MESH,
        )
        cp.start()
        t_copies.append(cp)

    def rank_copy(slot, target, sem):
        return pltpu.make_async_remote_copy(
            src_ref=rank.at[slot],
            dst_ref=rank.at[slot],
            send_sem=r_send.at[sem],
            recv_sem=r_recv.at[slot],
            device_id={"head": target},
            device_id_type=MESH,
        )

    sibling = hm + 1 - 2 * core
    loads["rf"].wait()
    rank_copies = []
    for k in range(CORES, n_head, CORES):
        rank_copies.append(rank_copy(hm, lax.rem(hm + k, n_head), k))
        rank_copies[-1].start()
    rank_copies.append(rank_copy(hm, sibling, 0))
    rank_copies[-1].start()

    loads["be"].wait()
    loads["iw"].wait()
    loads["ig"].wait()
    loads["k"].wait()
    loads["v"].wait()
    weight = iw[...]
    gain = ig[...]
    blocks = [(u, c) for u in range(users) for c in range(chunks)]
    for b, (u, c) in enumerate(blocks):
        r = slice(b * chunk, (b + 1) * chunk)
        rc = slice(c * chunk, (c + 1) * chunk)
        rows = normed(be[u, rc, :], weight, gain)
        norm_s[r, :] = rows
        key = (mm(rows, pw[1]) * DH ** (-0.5)).astype(BF16)
        val = mm(rows, pw[2]).astype(BF16)
        key_s[r, :] = key
        val_s[r, :] = val
        for h in range(heads):
            p = h * users + u
            hc = slice(h * DH, (h + 1) * DH)
            kw = (key[:, hc].astype(F32) * col[rc, 8 + p : 9 + p]).astype(BF16)
            lst[p, c] = mm_tn(kw, val[:, hc])
    for p in range(pairs):
        total = lst[p, 0]
        for c in range(1, chunks):
            total = total * fades[c][p : p + 1, :] + lst[p, c]
        loc[p] = total

    def right_copy(p):
        return pltpu.make_async_remote_copy(
            src_ref=p_out.at[p],
            dst_ref=p_in.at[p],
            send_sem=p_send.at[p],
            recv_sem=p_recv.at[p],
            device_id={"ctx": lax.rem(me + 1, n_ctx)},
            device_id_type=MESH,
        )

    def left_copy(p):
        return pltpu.make_async_remote_copy(
            src_ref=x_out.at[p],
            dst_ref=x_in.at[p],
            send_sem=x_send.at[p],
            recv_sem=x_recv.at[p],
            device_id={"ctx": lax.rem(me + n_ctx - 1, n_ctx)},
            device_id_type=MESH,
        )

    last = n_ctx - 1

    @pl.when(me == 0)
    def _():
        p_in[...] = jnp.zeros_like(p_in)
        for p in range(pairs):
            p_out[p] = loc[p].astype(p_out.dtype)
            if n_ctx > 1:
                right_copy(p).start()

    @pl.when(me == last)
    def _():
        x_in[...] = jnp.zeros_like(x_in)
        for p in range(pairs):
            x_out[p] = loc[p].astype(x_out.dtype)
            if n_ctx > 1:
                left_copy(p).start()

    loads["q"].wait()
    loads["g"].wait()
    loads["og"].wait()
    out_gain = og[...]
    for b in range(len(blocks)):
        r = slice(b * chunk, (b + 1) * chunk)
        rows = norm_s[r, :]
        qry_s[r, :] = mm(rows, pw[0]).astype(BF16)
        gate_s[r, :] = silu(mm(rows, pw[3]).astype(BF16).astype(F32)) * out_gain

    for k in range(1, n_ctx):
        src = lax.rem(me + n_ctx - k, n_ctx)
        pltpu.make_async_remote_copy(
            src_ref=tall.at[src],
            dst_ref=tall.at[src],
            send_sem=t_send.at[k],
            recv_sem=t_recv.at[src],
            device_id={"ctx": lax.rem(me + k, n_ctx)},
            device_id_type=MESH,
        ).wait_recv()
    after = jnp.zeros((8, 128), F32)
    for j in range(n_ctx):
        after = after + jnp.where(j > me, tall[j], 0.0)
    fade_after = jnp.exp(after)[:, 0:1]

    def relay_right():
        for p in range(pairs):
            right_copy(p).wait_recv()

            @pl.when(me < last)
            def _():
                p_out[p] = (
                    p_in[p].astype(F32) * fade_total[p : p + 1, :] + loc[p]
                ).astype(p_out.dtype)
                right_copy(p).start()

    def relay_left():
        for p in range(pairs):
            left_copy(p).wait_recv()

            @pl.when(me > 0)
            def _():
                x_out[p] = (
                    x_in[p].astype(F32) + loc[p] * fade_after[p : p + 1, :]
                ).astype(x_out.dtype)
                left_copy(p).start()

    half = n_ctx // 2
    if n_ctx > 1:

        @pl.when((me > 0) & (me < half))
        def _():
            relay_right()

        @pl.when((me < last) & (me >= half))
        def _():
            relay_left()

    tri = lax.broadcasted_iota(jnp.int32, (chunk, chunk), 0) >= lax.broadcasted_iota(
        jnp.int32, (chunk, chunk), 1
    )
    for b, (u, c) in enumerate(blocks):
        r = slice(b * chunk, (b + 1) * chunk)
        rc = slice(c * chunk, (c + 1) * chunk)
        seen = tri & (valid[u][:, rc] > 0.5)
        for h in range(heads):
            p = h * users + u
            hc = slice(h * DH, (h + 1) * DH)
            gap = col[rc, p : p + 1] - dat[p : p + 1, rc]
            decay = jnp.where(seen, jnp.exp(jnp.where(tri, gap, 0.0)), 0.0)
            att = (mm_nt(qry_s[r, hc], key_s[r, hc]) * decay).astype(BF16)
            within_s[r, hc] = mm(att, val_s[r, hc])

    loads["ce"].wait()
    loads["r2"].wait()
    cnorm[...] = normed(ce[...].reshape(users * cand, ce.shape[2]), weight, gain)
    cand_q = mm(cnorm[...], pw[0]).astype(BF16)
    own = cnorm[:, pl.ds(pl.multiple_of(hm * cols, DH), cols)].astype(F32)

    if n_ctx > 1:

        @pl.when((me < last) & (me < half))
        def _():
            relay_left()

        @pl.when((me > 0) & (me >= half))
        def _():
            relay_right()

    for p in range(pairs):
        h, u = p // users, p % users
        hc = slice(h * DH, (h + 1) * DH)
        rows = slice(u * cand, (u + 1) * cand)
        state = p_in[p].astype(F32) * fade_total[p : p + 1, :] + loc[p]
        state = state * fade_after[p : p + 1, :] + x_in[p].astype(F32)
        read = mm(cand_q[rows, hc], state.astype(BF16))
        scale = lax.rsqrt(jnp.mean(read * read, axis=-1, keepdims=True) + EPS)
        feat[u, :, hc] = (read * scale * out_gain[:, hc] + own[rows, hc]).astype(BF16)

    def feat_copy(k):
        target = lax.rem(hm + k, n_head)
        return pltpu.make_async_remote_copy(
            src_ref=feat.at[:, pl.ds(pl.multiple_of(target * share, share), share), :],
            dst_ref=feat_in.at[hm],
            send_sem=f_send.at[k],
            recv_sem=f_recv.at[hm],
            device_id={"head": target},
            device_id_type=MESH,
        )

    for k in range(1, n_head):
        feat_copy(k).start()

    for k in range(CORES, n_head, CORES):
        src = lax.rem(hm + n_head - k, n_head)
        rank_copy(src, sibling, k).wait_recv()
        rank_copies.append(rank_copy(src, sibling, n_head + k))
        rank_copies[-1].start()

    out_copies = []
    for u in range(users):
        for h in range(heads):
            p = h * users + u
            hc = slice(h * DH, (h + 1) * DH)
            state = p_in[p].astype(F32)
            for c in range(chunks):
                r = slice((u * chunks + c) * chunk, (u * chunks + c + 1) * chunk)
                rc = slice(c * chunk, (c + 1) * chunk)
                read = within_s[r, hc] + col[rc, 16 + p : 17 + p] * mm(
                    qry_s[r, hc], state.astype(BF16)
                )
                scale = lax.rsqrt(jnp.mean(read * read, axis=-1, keepdims=True) + EPS)
                hist[u, rc, hc] = (read * scale * gate_s[r, hc]).astype(BF16)
                if c + 1 < chunks:
                    state = state * fades[c][p : p + 1, :] + lst[p, c]
        out_copies.append(pltpu.make_async_copy(hist.at[u], hist_h.at[u], out_sem.at[u]))
        out_copies[-1].start()

    mine = feat[:, pl.ds(pl.multiple_of(hm * share, share), share), :]
    hidden = mm(mine.reshape(users * share, cols), rank[hm])
    rank_copy(sibling, sibling, 0).wait_recv()
    for k in range(CORES, n_head, CORES):
        src = lax.rem(sibling + n_head - k, n_head)
        rank_copy(src, sibling, n_head + k).wait_recv()
    for k in range(1, n_head):
        src = lax.rem(hm + n_head - k, n_head)
        pltpu.make_async_remote_copy(
            src_ref=feat_in.at[src],
            dst_ref=feat_in.at[src],
            send_sem=f_send.at[k],
            recv_sem=f_recv.at[src],
            device_id={"head": src},
            device_id_type=MESH,
        ).wait_recv()
        hidden = hidden + mm(feat_in[src].reshape(users * share, cols), rank[src])
    acted = silu(hidden) * r2[...].astype(F32)
    score_o[...] = jnp.sum(acted.reshape(users, share, acted.shape[1]), axis=-1)

    for cp in t_copies + rank_copies:
        cp.wait_send()
    for k in range(1, n_head):
        feat_copy(k).wait_send()
    if n_ctx > 1:

        @pl.when(me < last)
        def _():
            for p in range(pairs):
                right_copy(p).wait_send()

        @pl.when(me > 0)
        def _():
            for p in range(pairs):
                left_copy(p).wait_send()

    for cp in out_copies:
        cp.wait()


def local(
    n_ctx,
    n_head,
    behavior_embed,
    behavior_mask,
    history_len,
    log_decay,
    candidate_embed,
    input_weight,
    input_gain,
    proj_weight,
    output_gain,
    ranker_first,
    ranker_second,
):
    users, span, embed = behavior_embed.shape
    cand = candidate_embed.shape[1]
    width, cols = proj_weight.shape[1:]
    hidden = ranker_first.shape[1]
    heads = cols // DH
    pairs = heads * users
    chunk = 256 if span % 256 == 0 else 128
    chunks = span // chunk
    share = cand // n_head
    wire = BF16 if n_ctx <= 8 else F32
    rows = users * span
    dma = pltpu.SemaphoreType.DMA
    any_spec = pl.BlockSpec(memory_space=pl.ANY)
    flops = 2 * rows * width * (embed + 4 * cols)
    history_out, scores = pl.pallas_call(
        functools.partial(kernel, n_ctx, n_head, chunk),
        out_shape=(
            jax.ShapeDtypeStruct((users, span, cols), BF16),
            jax.ShapeDtypeStruct((users, share), F32),
        ),
        in_specs=[pl.BlockSpec(memory_space=pltpu.SMEM)] + [any_spec] * 10,
        out_specs=(any_spec, pl.BlockSpec(memory_space=pltpu.VMEM)),
        scratch_shapes=[
            pltpu.VMEM((users, span, embed), BF16),
            pltpu.VMEM((users, span), jnp.int32),
            pltpu.VMEM((heads, users, span), F32),
            pltpu.VMEM((users, cand, embed), BF16),
            pltpu.VMEM((embed, width), BF16),
            pltpu.VMEM((1, width), F32),
            pltpu.VMEM((4, width, cols), BF16),
            pltpu.VMEM((1, cols), F32),
            pltpu.VMEM((1, hidden), BF16),
            pltpu.VMEM((n_head, cols, hidden), BF16),
            pltpu.VMEM((rows, width), BF16),
            pltpu.VMEM((users * cand, width), BF16),
            pltpu.VMEM((rows, cols), BF16),
            pltpu.VMEM((rows, cols), BF16),
            pltpu.VMEM((rows, cols), BF16),
            pltpu.VMEM((rows, cols), F32),
            pltpu.VMEM((rows, cols), F32),
            pltpu.VMEM((users, span, cols), BF16),
            pltpu.VMEM((24, span), F32),
            pltpu.VMEM((pairs, chunks, DH, DH), F32),
            pltpu.VMEM((pairs, DH, DH), F32),
            pltpu.VMEM((n_ctx, 8, 128), F32),
            pltpu.VMEM((pairs, DH, DH), wire),
            pltpu.VMEM((pairs, DH, DH), wire),
            pltpu.VMEM((pairs, DH, DH), wire),
            pltpu.VMEM((pairs, DH, DH), wire),
            pltpu.VMEM((users, cand, cols), BF16),
            pltpu.VMEM((n_head, users, share, cols), BF16),
            dma((13,)),
            dma((users,)),
            dma((n_ctx,)),
            dma((n_ctx,)),
            dma((pairs,)),
            dma((pairs,)),
            dma((pairs,)),
            dma((pairs,)),
            dma((2 * n_head,)),
            dma((n_head,)),
            dma((n_head,)),
            dma((n_head,)),
        ],
        compiler_params=pltpu.CompilerParams(
            collective_id=0, has_side_effects=True, vmem_limit_bytes=48 * 1024 * 1024
        ),
        cost_estimate=pl.CostEstimate(
            flops=flops, bytes_accessed=6 * 1024 * 1024, transcendentals=0
        ),
    )(
        history_len,
        behavior_embed,
        behavior_mask,
        log_decay,
        candidate_embed,
        input_weight,
        input_gain.reshape(1, width),
        proj_weight,
        output_gain.reshape(1, cols),
        ranker_first,
        ranker_second.reshape(1, hidden),
    )
    return history_out, scores


def solution(mesh):
    in_specs = (
        P("grp", "ctx", None),
        P("grp", "ctx"),
        P("grp"),
        P("head", "grp", "ctx"),
        P("grp", "ctx", None),
        P(),
        P(),
        P(None, None, "head"),
        P("head"),
        P("head", None),
        P(),
    )
    out_specs = (P("grp", "ctx", "head"), P("grp", ("ctx", "head")))
    return jax.shard_map(
        functools.partial(local, mesh.shape["ctx"], mesh.shape["head"]),
        mesh=mesh,
        in_specs=in_specs,
        out_specs=out_specs,
        check_vma=False,
    )
```

```python
import functools

import jax
import jax.numpy as jnp
from jax import lax
from jax.experimental import pallas as pl
from jax.experimental.pallas import tpu as pltpu
from jax.sharding import PartitionSpec as P

DH = 128
CORES = 2
EPS = 1e-05
F32 = jnp.float32
BF16 = jnp.bfloat16
MESH = pl.DeviceIdType.MESH


def mm(a, b):
    return jnp.dot(a, b, preferred_element_type=F32)


def mm_tn(a, b):
    return lax.dot_general(a, b, (((0,), (0,)), ((), ())), preferred_element_type=F32)


def mm_nt(a, b):
    return lax.dot_general(a, b, (((1,), (1,)), ((), ())), preferred_element_type=F32)


def silu(x):
    return x / (1.0 + jnp.exp(-x))


def normed(rows, weight, gain):
    raw = mm(rows, weight).astype(BF16).astype(F32)
    scale = lax.rsqrt(jnp.mean(raw * raw, axis=-1, keepdims=True) + EPS)
    return (raw * scale * gain).astype(BF16)


def kernel(
    n_ctx,
    n_head,
    chunk,
    hl,
    be_h,
    mk_h,
    ld_h,
    ce_h,
    iw_h,
    ig_h,
    pw_h,
    og_h,
    rf_h,
    r2_h,
    hist_h,
    score_o,
    be,
    mk,
    ld,
    ce,
    iw,
    ig,
    pw,
    og,
    r2,
    rank,
    norm_s,
    cnorm,
    key_s,
    val_s,
    qry_s,
    gate_s,
    within_s,
    hist,
    dat,
    lst,
    loc,
    tall,
    p_in,
    p_out,
    x_in,
    x_out,
    feat,
    feat_in,
    load_sem,
    out_sem,
    t_send,
    t_recv,
    p_send,
    p_recv,
    x_send,
    x_recv,
    r_send,
    r_recv,
    f_send,
    f_recv,
):
    users, span, _ = be.shape
    cand = ce.shape[1]
    cols = og.shape[1]
    heads = cols // DH
    pairs = heads * users
    chunks = span // chunk
    share = cand // n_head
    me = lax.axis_index("ctx")
    hm = lax.axis_index("head")
    core = lax.rem(hm, CORES)

    loads = {}
    for i, (name, src, dst) in enumerate(
        (
            ("rf", rf_h, rank.at[hm]),
            ("be", be_h, be),
            ("iw", iw_h, iw),
            ("ig", ig_h, ig),
            ("ld", ld_h, ld),
            ("mk", mk_h, mk),
            ("k", pw_h.at[1], pw.at[1]),
            ("v", pw_h.at[2], pw.at[2]),
            ("q", pw_h.at[0], pw.at[0]),
            ("g", pw_h.at[3], pw.at[3]),
            ("og", og_h, og),
            ("ce", ce_h, ce),
            ("r2", r2_h, r2),
        )
    ):
        loads[name] = pltpu.make_async_copy(src, dst, load_sem.at[i])
        loads[name].start()

    barrier = pltpu.get_barrier_semaphore()
    for k in range(1, n_ctx):
        pl.semaphore_signal(
            barrier, inc=1, device_id={"ctx": lax.rem(me + k, n_ctx)}, device_id_type=MESH
        )
    for k in range(1, n_head):
        pl.semaphore_signal(
            barrier, inc=1, device_id={"head": lax.rem(hm + k, n_head)}, device_id_type=MESH
        )

    pl.semaphore_wait(barrier, n_ctx + n_head - 2)

    def rank_copy(slot, target, sem):
        return pltpu.make_async_remote_copy(
            src_ref=rank.at[slot],
            dst_ref=rank.at[slot],
            send_sem=r_send.at[sem],
            recv_sem=r_recv.at[slot],
            device_id={"head": target},
            device_id_type=MESH,
        )

    sibling = hm + 1 - 2 * core
    loads["rf"].wait()
    rank_copies = []
    for k in range(CORES, n_head, CORES):
        rank_copies.append(rank_copy(hm, lax.rem(hm + k, n_head), k))
        rank_copies[-1].start()
    rank_copies.append(rank_copy(hm, sibling, 0))
    rank_copies[-1].start()

    loads["ld"].wait()
    loads["mk"].wait()
    dat[...] = jnp.zeros_like(dat)
    for u in range(users):
        for h in range(heads):
            p = u * heads + h
            dat[p : p + 1, :] = ld[h, u : u + 1, :]
    cum = dat[0:8, :]
    lane = lax.broadcasted_iota(jnp.int32, (8, span), 1)
    in_chunk = lax.rem(lane, chunk)
    step = 1
    while step < chunk:
        cum = cum + jnp.where(in_chunk >= step, pltpu.roll(cum, step, 1), 0.0)
        step *= 2
    ends = [cum[:, (c + 1) * chunk - 1 : (c + 1) * chunk] for c in range(chunks)]
    fades = [jnp.exp(e) for e in ends]
    end_total = functools.reduce(jnp.add, ends)
    fade_total = jnp.exp(end_total)
    end_row = ends[-1]
    for c in range(chunks - 2, -1, -1):
        end_row = jnp.where(lane < (c + 1) * chunk, ends[c], end_row)
    weight_rows = jnp.exp(end_row - cum)
    dat[0:8, :] = cum
    dat[8:16, :] = weight_rows
    dat[16:24, :] = jnp.exp(cum)
    pos = me * span + lax.broadcasted_iota(jnp.int32, (1, span), 1)
    valid = []
    for u in range(users):
        keep = (pos >= n_ctx * span - hl[u]) & (mk[u : u + 1, :] == 1)
        valid.append(jnp.where(keep, 1.0, 0.0))
    for h in range(heads):
        for u in range(users):
            p = 8 + u * heads + h
            dat[p : p + 1, :] = dat[p : p + 1, :] * valid[u]
    col = jnp.transpose(dat[...])
    tall[me] = jnp.broadcast_to(end_total, (8, 128))

    t_copies = []
    for k in range(1, n_ctx):
        cp = pltpu.make_async_remote_copy(
            src_ref=tall.at[me],
            dst_ref=tall.at[me],
            send_sem=t_send.at[k],
            recv_sem=t_recv.at[me],
            device_id={"ctx": lax.rem(me + k, n_ctx)},
            device_id_type=MESH,
        )
        cp.start()
        t_copies.append(cp)

    def right_copy(p):
        return pltpu.make_async_remote_copy(
            src_ref=p_out.at[p],
            dst_ref=p_in.at[p],
            send_sem=p_send.at[p],
            recv_sem=p_recv.at[p],
            device_id={"ctx": lax.rem(me + 1, n_ctx)},
            device_id_type=MESH,
        )

    def left_copy(p):
        return pltpu.make_async_remote_copy(
            src_ref=x_out.at[p],
            dst_ref=x_in.at[p],
            send_sem=x_send.at[p],
            recv_sem=x_recv.at[p],
            device_id={"ctx": lax.rem(me + n_ctx - 1, n_ctx)},
            device_id_type=MESH,
        )

    last = n_ctx - 1

    @pl.when(me == 0)
    def _():
        p_in[...] = jnp.zeros_like(p_in)

    @pl.when(me == last)
    def _():
        x_in[...] = jnp.zeros_like(x_in)

    loads["be"].wait()
    loads["iw"].wait()
    loads["ig"].wait()
    loads["k"].wait()
    loads["v"].wait()
    weight = iw[...]
    gain = ig[...]
    blocks = [(u, c) for u in range(users) for c in range(chunks)]
    for u in range(users):
        for c in range(chunks):
            b = u * chunks + c
            r = slice(b * chunk, (b + 1) * chunk)
            rc = slice(c * chunk, (c + 1) * chunk)
            rows = normed(be[u, rc, :], weight, gain)
            norm_s[r, :] = rows
            key = (mm(rows, pw[1]) * DH ** (-0.5)).astype(BF16)
            val = mm(rows, pw[2]).astype(BF16)
            key_s[r, :] = key
            val_s[r, :] = val
            for h in range(heads):
                p = u * heads + h
                hc = slice(h * DH, (h + 1) * DH)
                kw = (key[:, hc].astype(F32) * col[rc, 8 + p : 9 + p]).astype(BF16)
                lst[p, c] = mm_tn(kw, val[:, hc])
        mine = range(u * heads, (u + 1) * heads)
        for p in mine:
            total = lst[p, 0]
            for c in range(1, chunks):
                total = total * fades[c][p : p + 1, :] + lst[p, c]
            loc[p] = total

        @pl.when(me == 0)
        def _():
            for p in mine:
                p_out[p] = loc[p].astype(p_out.dtype)
                if n_ctx > 1:
                    right_copy(p).start()

        @pl.when(me == last)
        def _():
            for p in mine:
                x_out[p] = loc[p].astype(x_out.dtype)
                if n_ctx > 1:
                    left_copy(p).start()

    loads["q"].wait()
    loads["g"].wait()
    loads["og"].wait()
    out_gain = og[...]
    for b in range(len(blocks)):
        r = slice(b * chunk, (b + 1) * chunk)
        rows = norm_s[r, :]
        qry_s[r, :] = mm(rows, pw[0]).astype(BF16)
        gate_s[r, :] = silu(mm(rows, pw[3]).astype(BF16).astype(F32)) * out_gain

    for k in range(1, n_ctx):
        src = lax.rem(me + n_ctx - k, n_ctx)
        pltpu.make_async_remote_copy(
            src_ref=tall.at[src],
            dst_ref=tall.at[src],
            send_sem=t_send.at[k],
            recv_sem=t_recv.at[src],
            device_id={"ctx": lax.rem(me + k, n_ctx)},
            device_id_type=MESH,
        ).wait_recv()
    after = jnp.zeros((8, 128), F32)
    for j in range(n_ctx):
        after = after + jnp.where(j > me, tall[j], 0.0)
    fade_after = jnp.exp(after)[:, 0:1]

    def relay_right():
        for p in range(pairs):
            right_copy(p).wait_recv()

            @pl.when(me < last)
            def _():
                p_out[p] = (
                    p_in[p].astype(F32) * fade_total[p : p + 1, :] + loc[p]
                ).astype(p_out.dtype)
                right_copy(p).start()

    def relay_left():
        for p in range(pairs):
            left_copy(p).wait_recv()

            @pl.when(me > 0)
            def _():
                x_out[p] = (
                    x_in[p].astype(F32) + loc[p] * fade_after[p : p + 1, :]
                ).astype(x_out.dtype)
                left_copy(p).start()

    half = n_ctx // 2
    if n_ctx > 1:

        @pl.when((me > 0) & (me < half))
        def _():
            relay_right()

        @pl.when((me < last) & (me >= half))
        def _():
            relay_left()

    tri = lax.broadcasted_iota(jnp.int32, (chunk, chunk), 0) >= lax.broadcasted_iota(
        jnp.int32, (chunk, chunk), 1
    )
    for b, (u, c) in enumerate(blocks):
        r = slice(b * chunk, (b + 1) * chunk)
        rc = slice(c * chunk, (c + 1) * chunk)
        seen = tri & (valid[u][:, rc] > 0.5)
        for h in range(heads):
            p = u * heads + h
            hc = slice(h * DH, (h + 1) * DH)
            gap = col[rc, p : p + 1] - dat[p : p + 1, rc]
            decay = jnp.where(seen, jnp.exp(jnp.where(tri, gap, 0.0)), 0.0)
            att = (mm_nt(qry_s[r, hc], key_s[r, hc]) * decay).astype(BF16)
            within_s[r, hc] = mm(att, val_s[r, hc])

    loads["ce"].wait()
    loads["r2"].wait()
    cnorm[...] = normed(ce[...].reshape(users * cand, ce.shape[2]), weight, gain)
    cand_q = mm(cnorm[...], pw[0]).astype(BF16)
    own = cnorm[:, pl.ds(pl.multiple_of(hm * cols, DH), cols)].astype(F32)

    if n_ctx > 1:

        @pl.when((me < last) & (me < half))
        def _():
            relay_left()

        @pl.when((me > 0) & (me >= half))
        def _():
            relay_right()

    for p in range(pairs):
        u, h = p // heads, p % heads
        hc = slice(h * DH, (h + 1) * DH)
        rows = slice(u * cand, (u + 1) * cand)
        state = p_in[p].astype(F32) * fade_total[p : p + 1, :] + loc[p]
        state = state * fade_after[p : p + 1, :] + x_in[p].astype(F32)
        read = mm(cand_q[rows, hc], state.astype(BF16))
        scale = lax.rsqrt(jnp.mean(read * read, axis=-1, keepdims=True) + EPS)
        feat[u, :, hc] = (read * scale * out_gain[:, hc] + own[rows, hc]).astype(BF16)

    def feat_copy(k):
        target = lax.rem(hm + k, n_head)
        return pltpu.make_async_remote_copy(
            src_ref=feat.at[:, pl.ds(pl.multiple_of(target * share, share), share), :],
            dst_ref=feat_in.at[hm],
            send_sem=f_send.at[k],
            recv_sem=f_recv.at[hm],
            device_id={"head": target},
            device_id_type=MESH,
        )

    for k in range(1, n_head):
        feat_copy(k).start()

    for k in range(CORES, n_head, CORES):
        src = lax.rem(hm + n_head - k, n_head)
        rank_copy(src, sibling, k).wait_recv()
        rank_copies.append(rank_copy(src, sibling, n_head + k))
        rank_copies[-1].start()

    out_copies = []
    for u in range(users):
        for h in range(heads):
            p = u * heads + h
            hc = slice(h * DH, (h + 1) * DH)
            state = p_in[p].astype(F32)
            for c in range(chunks):
                r = slice((u * chunks + c) * chunk, (u * chunks + c + 1) * chunk)
                rc = slice(c * chunk, (c + 1) * chunk)
                read = within_s[r, hc] + col[rc, 16 + p : 17 + p] * mm(
                    qry_s[r, hc], state.astype(BF16)
                )
                scale = lax.rsqrt(jnp.mean(read * read, axis=-1, keepdims=True) + EPS)
                hist[u, rc, hc] = (read * scale * gate_s[r, hc]).astype(BF16)
                if c + 1 < chunks:
                    state = state * fades[c][p : p + 1, :] + lst[p, c]
        out_copies.append(pltpu.make_async_copy(hist.at[u], hist_h.at[u], out_sem.at[u]))
        out_copies[-1].start()

    mine = feat[:, pl.ds(pl.multiple_of(hm * share, share), share), :]
    hidden = mm(mine.reshape(users * share, cols), rank[hm])
    rank_copy(sibling, sibling, 0).wait_recv()
    for k in range(CORES, n_head, CORES):
        src = lax.rem(sibling + n_head - k, n_head)
        rank_copy(src, sibling, n_head + k).wait_recv()
    for k in range(1, n_head):
        src = lax.rem(hm + n_head - k, n_head)
        pltpu.make_async_remote_copy(
            src_ref=feat_in.at[src],
            dst_ref=feat_in.at[src],
            send_sem=f_send.at[k],
            recv_sem=f_recv.at[src],
            device_id={"head": src},
            device_id_type=MESH,
        ).wait_recv()
        hidden = hidden + mm(feat_in[src].reshape(users * share, cols), rank[src])
    second = r2[...].astype(F32)
    acted = silu(hidden)
    summed = acted[:, 0:128] * second[0:1, :]
    for i in range(1, second.shape[0]):
        summed = summed + acted[:, i * 128 : (i + 1) * 128] * second[i : i + 1, :]
    score_o[...] = jnp.sum(summed.reshape(users, share, 128), axis=-1)

    for cp in t_copies + rank_copies:
        cp.wait_send()
    for k in range(1, n_head):
        feat_copy(k).wait_send()
    if n_ctx > 1:

        @pl.when(me < last)
        def _():
            for p in range(pairs):
                right_copy(p).wait_send()

        @pl.when(me > 0)
        def _():
            for p in range(pairs):
                left_copy(p).wait_send()

    for cp in out_copies:
        cp.wait()


def local(
    n_ctx,
    n_head,
    behavior_embed,
    behavior_mask,
    history_len,
    log_decay,
    candidate_embed,
    input_weight,
    input_gain,
    proj_weight,
    output_gain,
    ranker_first,
    ranker_second,
):
    users, span, embed = behavior_embed.shape
    cand = candidate_embed.shape[1]
    width, cols = proj_weight.shape[1:]
    hidden = ranker_first.shape[1]
    heads = cols // DH
    pairs = heads * users
    chunk = 256 if span % 256 == 0 else 128
    chunks = span // chunk
    share = cand // n_head
    wire = BF16 if n_ctx <= 8 else F32
    rows = users * span
    dma = pltpu.SemaphoreType.DMA
    hbm_spec = pl.BlockSpec(memory_space=pltpu.HBM)
    vmem_spec = pl.BlockSpec(memory_space=pltpu.VMEM)
    flops = 2 * rows * width * (embed + 4 * cols)
    history_out, scores = pl.pallas_call(
        functools.partial(kernel, n_ctx, n_head, chunk),
        out_shape=(
            jax.ShapeDtypeStruct((users, span, cols), BF16),
            jax.ShapeDtypeStruct((users, share), F32),
        ),
        in_specs=[pl.BlockSpec(memory_space=pltpu.SMEM)] + [hbm_spec] * 10,
        out_specs=(hbm_spec, vmem_spec),
        scratch_shapes=[
            pltpu.VMEM((users, span, embed), BF16),
            pltpu.VMEM((users, span), jnp.int32),
            pltpu.VMEM((heads, users, span), F32),
            pltpu.VMEM((users, cand, embed), BF16),
            pltpu.VMEM((embed, width), BF16),
            pltpu.VMEM((1, width), F32),
            pltpu.VMEM((4, width, cols), BF16),
            pltpu.VMEM((1, cols), F32),
            pltpu.VMEM((hidden // 128, 128), BF16),
            pltpu.VMEM((n_head, cols, hidden), BF16),
            pltpu.VMEM((rows, width), BF16),
            pltpu.VMEM((users * cand, width), BF16),
            pltpu.VMEM((rows, cols), BF16),
            pltpu.VMEM((rows, cols), BF16),
            pltpu.VMEM((rows, cols), BF16),
            pltpu.VMEM((rows, cols), F32),
            pltpu.VMEM((rows, cols), F32),
            pltpu.VMEM((users, span, cols), BF16),
            pltpu.VMEM((24, span), F32),
            pltpu.VMEM((pairs, chunks, DH, DH), F32),
            pltpu.VMEM((pairs, DH, DH), F32),
            pltpu.VMEM((n_ctx, 8, 128), F32),
            pltpu.VMEM((pairs, DH, DH), wire),
            pltpu.VMEM((pairs, DH, DH), wire),
            pltpu.VMEM((pairs, DH, DH), wire),
            pltpu.VMEM((pairs, DH, DH), wire),
            pltpu.VMEM((users, cand, cols), BF16),
            pltpu.VMEM((n_head, users, share, cols), BF16),
            dma((13,)),
            dma((users,)),
            dma((n_ctx,)),
            dma((n_ctx,)),
            dma((pairs,)),
            dma((pairs,)),
            dma((pairs,)),
            dma((pairs,)),
            dma((2 * n_head,)),
            dma((n_head,)),
            dma((n_head,)),
            dma((n_head,)),
        ],
        compiler_params=pltpu.CompilerParams(
            collective_id=0, has_side_effects=True, vmem_limit_bytes=60 * 1024 * 1024
        ),
        cost_estimate=pl.CostEstimate(
            flops=flops, bytes_accessed=6 * 1024 * 1024, transcendentals=0
        ),
    )(
        history_len,
        behavior_embed,
        behavior_mask,
        log_decay,
        candidate_embed,
        input_weight,
        input_gain.reshape(1, width),
        proj_weight,
        output_gain.reshape(1, cols),
        ranker_first,
        ranker_second.reshape(hidden // 128, 128),
    )
    return history_out, scores


def solution(mesh):
    in_specs = (
        P("grp", "ctx", None),
        P("grp", "ctx"),
        P("grp"),
        P("head", "grp", "ctx"),
        P("grp", "ctx", None),
        P(),
        P(),
        P(None, None, "head"),
        P("head"),
        P("head", None),
        P(),
    )
    out_specs = (P("grp", "ctx", "head"), P("grp", ("ctx", "head")))
    return jax.shard_map(
        functools.partial(local, mesh.shape["ctx"], mesh.shape["head"]),
        mesh=mesh,
        in_specs=in_specs,
        out_specs=out_specs,
        check_vma=False,
    )
```

```python
import functools

import jax
import jax.numpy as jnp
from jax import lax
from jax.experimental import pallas as pl
from jax.experimental.pallas import tpu as pltpu
from jax.sharding import PartitionSpec as P

DH = 128
CORES = 2
EPS = 1e-05
F32 = jnp.float32
BF16 = jnp.bfloat16
MESH = pl.DeviceIdType.MESH


def mm(a, b):
    return jnp.dot(a, b, preferred_element_type=F32)


def mm_tn(a, b):
    return lax.dot_general(a, b, (((0,), (0,)), ((), ())), preferred_element_type=F32)


def mm_nt(a, b):
    return lax.dot_general(a, b, (((1,), (1,)), ((), ())), preferred_element_type=F32)


def silu(x):
    return x / (1.0 + jnp.exp(-x))


def normed(rows, weight, gain):
    raw = mm(rows, weight).astype(BF16).astype(F32)
    scale = lax.rsqrt(jnp.mean(raw * raw, axis=-1, keepdims=True) + EPS)
    return (raw * scale * gain).astype(BF16)


def kernel(
    n_ctx,
    n_head,
    chunk,
    hl,
    be_h,
    mk_h,
    ld_h,
    ce_h,
    iw_h,
    ig_h,
    pw_h,
    og_h,
    rf_h,
    r2_h,
    hist_h,
    score_o,
    be,
    mk,
    ld,
    ce,
    iw,
    ig,
    pw,
    og,
    r2,
    rank,
    norm_s,
    cnorm,
    key_s,
    val_s,
    qry_s,
    gate_s,
    within_s,
    hist,
    dat,
    lst,
    loc,
    tall,
    p_in,
    p_out,
    x_in,
    x_out,
    feat,
    feat_in,
    load_sem,
    out_sem,
    t_send,
    t_recv,
    p_send,
    p_recv,
    x_send,
    x_recv,
    r_send,
    r_recv,
    f_send,
    f_recv,
):
    users, span, _ = be.shape
    cand = ce.shape[1]
    cols = og.shape[1]
    heads = cols // DH
    pairs = heads * users
    chunks = span // chunk
    share = cand // n_head
    me = lax.axis_index("ctx")
    hm = lax.axis_index("head")
    core = lax.rem(hm, CORES)

    loads = {}
    for i, (name, src, dst) in enumerate(
        (
            ("rf", rf_h, rank.at[hm]),
            ("be", be_h, be),
            ("iw", iw_h, iw),
            ("ig", ig_h, ig),
            ("ld", ld_h, ld),
            ("mk", mk_h, mk),
            ("k", pw_h.at[1], pw.at[1]),
            ("v", pw_h.at[2], pw.at[2]),
            ("q", pw_h.at[0], pw.at[0]),
            ("g", pw_h.at[3], pw.at[3]),
            ("og", og_h, og),
            ("ce", ce_h, ce),
            ("r2", r2_h, r2),
        )
    ):
        loads[name] = pltpu.make_async_copy(src, dst, load_sem.at[i])
        loads[name].start()

    barrier = pltpu.get_barrier_semaphore()
    for k in range(1, n_ctx):
        pl.semaphore_signal(
            barrier, inc=1, device_id={"ctx": lax.rem(me + k, n_ctx)}, device_id_type=MESH
        )
    for k in range(1, n_head):
        pl.semaphore_signal(
            barrier, inc=1, device_id={"head": lax.rem(hm + k, n_head)}, device_id_type=MESH
        )

    for name in ("ld", "mk", "be", "iw", "ig", "k", "v"):
        loads[name].wait()
    dat[...] = jnp.zeros_like(dat)
    for u in range(users):
        for h in range(heads):
            p = u * heads + h
            dat[p : p + 1, :] = ld[h, u : u + 1, :]
    cum = dat[0:8, :]
    lane = lax.broadcasted_iota(jnp.int32, (8, span), 1)
    in_chunk = lax.rem(lane, chunk)
    step = 1
    while step < chunk:
        cum = cum + jnp.where(in_chunk >= step, pltpu.roll(cum, step, 1), 0.0)
        step *= 2
    ends = [cum[:, (c + 1) * chunk - 1 : (c + 1) * chunk] for c in range(chunks)]
    fades = [jnp.exp(e) for e in ends]
    end_total = functools.reduce(jnp.add, ends)
    fade_total = jnp.exp(end_total)
    end_row = ends[-1]
    for c in range(chunks - 2, -1, -1):
        end_row = jnp.where(lane < (c + 1) * chunk, ends[c], end_row)
    weight_rows = jnp.exp(end_row - cum)
    dat[0:8, :] = cum
    dat[8:16, :] = weight_rows
    dat[16:24, :] = jnp.exp(cum)
    pos = me * span + lax.broadcasted_iota(jnp.int32, (1, span), 1)
    valid = []
    for u in range(users):
        keep = (pos >= n_ctx * span - hl[u]) & (mk[u : u + 1, :] == 1)
        valid.append(jnp.where(keep, 1.0, 0.0))
    for h in range(heads):
        for u in range(users):
            p = 8 + u * heads + h
            dat[p : p + 1, :] = dat[p : p + 1, :] * valid[u]
    col = jnp.transpose(dat[...])
    tall[me] = jnp.broadcast_to(end_total, (8, 128))

    def right_copy(p):
        return pltpu.make_async_remote_copy(
            src_ref=p_out.at[p],
            dst_ref=p_in.at[p],
            send_sem=p_send.at[p],
            recv_sem=p_recv.at[p],
            device_id={"ctx": lax.rem(me + 1, n_ctx)},
            device_id_type=MESH,
        )

    def left_copy(p):
        return pltpu.make_async_remote_copy(
            src_ref=x_out.at[p],
            dst_ref=x_in.at[p],
            send_sem=x_send.at[p],
            recv_sem=x_recv.at[p],
            device_id={"ctx": lax.rem(me + n_ctx - 1, n_ctx)},
            device_id_type=MESH,
        )

    last = n_ctx - 1

    weight = iw[...]
    gain = ig[...]
    tri = lax.broadcasted_iota(jnp.int32, (chunk, chunk), 0) >= lax.broadcasted_iota(
        jnp.int32, (chunk, chunk), 1
    )

    def place(u, c):
        b = u * chunks + c
        return slice(b * chunk, (b + 1) * chunk), slice(c * chunk, (c + 1) * chunk)

    def keys_values(u, c):
        r, rc = place(u, c)
        rows = normed(be[u, rc, :], weight, gain)
        norm_s[r, :] = rows
        key = (mm(rows, pw[1]) * DH ** (-0.5)).astype(BF16)
        val = mm(rows, pw[2]).astype(BF16)
        key_s[r, :] = key
        val_s[r, :] = val
        for h in range(heads):
            p = u * heads + h
            hc = slice(h * DH, (h + 1) * DH)
            kw = (key[:, hc].astype(F32) * col[rc, 8 + p : 9 + p]).astype(BF16)
            lst[p, c] = mm_tn(kw, val[:, hc])

    def local_states(u):
        for p in range(u * heads, (u + 1) * heads):
            total = lst[p, 0]
            for c in range(1, chunks):
                total = total * fades[c][p : p + 1, :] + lst[p, c]
            loc[p] = total

    def first_sends(u):
        @pl.when(me == 0)
        def _():
            for p in range(u * heads, (u + 1) * heads):
                p_out[p] = loc[p].astype(p_out.dtype)
                if n_ctx > 1:
                    right_copy(p).start()

        @pl.when(me == last)
        def _():
            for p in range(u * heads, (u + 1) * heads):
                x_out[p] = loc[p].astype(x_out.dtype)
                if n_ctx > 1:
                    left_copy(p).start()

    def relay_right(u):
        for p in range(u * heads, (u + 1) * heads):
            right_copy(p).wait_recv()

            @pl.when(me < last)
            def _():
                p_out[p] = (
                    p_in[p].astype(F32) * fade_total[p : p + 1, :] + loc[p]
                ).astype(p_out.dtype)
                right_copy(p).start()

    def relay_left(u):
        for p in range(u * heads, (u + 1) * heads):
            left_copy(p).wait_recv()

            @pl.when(me > 0)
            def _():
                x_out[p] = (
                    x_in[p].astype(F32) + loc[p] * fade_after[p : p + 1, :]
                ).astype(x_out.dtype)
                left_copy(p).start()

    half = n_ctx // 2

    def near_relay(u):
        if n_ctx > 1:

            @pl.when((me > 0) & (me < half))
            def _():
                relay_right(u)

            @pl.when((me < last) & (me >= half))
            def _():
                relay_left(u)

    def far_relay(u, ends):
        if n_ctx > 1:
            at_end = (me == 0) | (me == last)
            turn = at_end if ends else jnp.logical_not(at_end)

            @pl.when(turn & (me < half))
            def _():
                relay_left(u)

            @pl.when(turn & (me >= half))
            def _():
                relay_right(u)

    def queries_gates(u):
        for c in range(chunks):
            r, _ = place(u, c)
            rows = norm_s[r, :]
            qry_s[r, :] = mm(rows, pw[0]).astype(BF16)
            gate_s[r, :] = silu(mm(rows, pw[3]).astype(BF16).astype(F32)) * out_gain

    def attention(u):
        for c in range(chunks):
            r, rc = place(u, c)
            seen = tri & (valid[u][:, rc] > 0.5)
            for h in range(heads):
                p = u * heads + h
                hc = slice(h * DH, (h + 1) * DH)
                gap = col[rc, p : p + 1] - dat[p : p + 1, rc]
                decay = jnp.where(seen, jnp.exp(jnp.where(tri, gap, 0.0)), 0.0)
                att = (mm_nt(qry_s[r, hc], key_s[r, hc]) * decay).astype(BF16)
                within_s[r, hc] = mm(att, val_s[r, hc])

    keys_values(0, 0)

    pl.semaphore_wait(barrier, n_ctx + n_head - 2)

    @pl.when(me == 0)
    def _():
        p_in[...] = jnp.zeros_like(p_in)

    @pl.when(me == last)
    def _():
        x_in[...] = jnp.zeros_like(x_in)

    t_copies = []
    for k in range(1, n_ctx):
        cp = pltpu.make_async_remote_copy(
            src_ref=tall.at[me],
            dst_ref=tall.at[me],
            send_sem=t_send.at[k],
            recv_sem=t_recv.at[me],
            device_id={"ctx": lax.rem(me + k, n_ctx)},
            device_id_type=MESH,
        )
        cp.start()
        t_copies.append(cp)

    def rank_copy(slot, target, sem):
        return pltpu.make_async_remote_copy(
            src_ref=rank.at[slot],
            dst_ref=rank.at[slot],
            send_sem=r_send.at[sem],
            recv_sem=r_recv.at[slot],
            device_id={"head": target},
            device_id_type=MESH,
        )

    sibling = hm + 1 - 2 * core
    loads["rf"].wait()
    rank_copies = []
    for k in range(CORES, n_head, CORES):
        rank_copies.append(rank_copy(hm, lax.rem(hm + k, n_head), k))
        rank_copies[-1].start()
    rank_copies.append(rank_copy(hm, sibling, 0))
    rank_copies[-1].start()

    for u in range(users):
        for c in range(chunks):
            if u + c > 0:
                keys_values(u, c)
        local_states(u)
        first_sends(u)

    for k in range(1, n_ctx):
        src = lax.rem(me + n_ctx - k, n_ctx)
        pltpu.make_async_remote_copy(
            src_ref=tall.at[src],
            dst_ref=tall.at[src],
            send_sem=t_send.at[k],
            recv_sem=t_recv.at[src],
            device_id={"ctx": lax.rem(me + k, n_ctx)},
            device_id_type=MESH,
        ).wait_recv()
    after = jnp.zeros((8, 128), F32)
    for j in range(n_ctx):
        after = after + jnp.where(j > me, tall[j], 0.0)
    fade_after = jnp.exp(after)[:, 0:1]

    for name in ("q", "g", "og", "ce", "r2"):
        loads[name].wait()
    out_gain = og[...]
    near_relay(0)
    for u in range(users):
        queries_gates(u)
        if u + 1 < users:
            near_relay(u + 1)
    far_relay(0, False)
    for u in range(users):
        attention(u)
        if u + 1 < users:
            far_relay(u + 1, False)
    cnorm[...] = normed(ce[...].reshape(users * cand, ce.shape[2]), weight, gain)
    cand_q = mm(cnorm[...], pw[0]).astype(BF16)
    own = cnorm[:, pl.ds(pl.multiple_of(hm * cols, DH), cols)].astype(F32)
    for u in range(users):
        far_relay(u, True)

    for p in range(pairs):
        u, h = p // heads, p % heads
        hc = slice(h * DH, (h + 1) * DH)
        rows = slice(u * cand, (u + 1) * cand)
        state = p_in[p].astype(F32) * fade_total[p : p + 1, :] + loc[p]
        state = state * fade_after[p : p + 1, :] + x_in[p].astype(F32)
        read = mm(cand_q[rows, hc], state.astype(BF16))
        scale = lax.rsqrt(jnp.mean(read * read, axis=-1, keepdims=True) + EPS)
        feat[u, :, hc] = (read * scale * out_gain[:, hc] + own[rows, hc]).astype(BF16)

    def feat_copy(k):
        target = lax.rem(hm + k, n_head)
        return pltpu.make_async_remote_copy(
            src_ref=feat.at[:, pl.ds(pl.multiple_of(target * share, share), share), :],
            dst_ref=feat_in.at[hm],
            send_sem=f_send.at[k],
            recv_sem=f_recv.at[hm],
            device_id={"head": target},
            device_id_type=MESH,
        )

    for k in range(1, n_head):
        feat_copy(k).start()

    for k in range(CORES, n_head, CORES):
        src = lax.rem(hm + n_head - k, n_head)
        rank_copy(src, sibling, k).wait_recv()
        rank_copies.append(rank_copy(src, sibling, n_head + k))
        rank_copies[-1].start()

    out_copies = []
    for u in range(users):
        for h in range(heads):
            p = u * heads + h
            hc = slice(h * DH, (h + 1) * DH)
            state = p_in[p].astype(F32)
            for c in range(chunks):
                r = slice((u * chunks + c) * chunk, (u * chunks + c + 1) * chunk)
                rc = slice(c * chunk, (c + 1) * chunk)
                read = within_s[r, hc] + col[rc, 16 + p : 17 + p] * mm(
                    qry_s[r, hc], state.astype(BF16)
                )
                scale = lax.rsqrt(jnp.mean(read * read, axis=-1, keepdims=True) + EPS)
                hist[u, rc, hc] = (read * scale * gate_s[r, hc]).astype(BF16)
                if c + 1 < chunks:
                    state = state * fades[c][p : p + 1, :] + lst[p, c]
        out_copies.append(pltpu.make_async_copy(hist.at[u], hist_h.at[u], out_sem.at[u]))
        out_copies[-1].start()

    mine = feat[:, pl.ds(pl.multiple_of(hm * share, share), share), :]
    hidden = mm(mine.reshape(users * share, cols), rank[hm])
    rank_copy(sibling, sibling, 0).wait_recv()
    for k in range(CORES, n_head, CORES):
        src = lax.rem(sibling + n_head - k, n_head)
        rank_copy(src, sibling, n_head + k).wait_recv()
    for k in range(1, n_head):
        src = lax.rem(hm + n_head - k, n_head)
        pltpu.make_async_remote_copy(
            src_ref=feat_in.at[src],
            dst_ref=feat_in.at[src],
            send_sem=f_send.at[k],
            recv_sem=f_recv.at[src],
            device_id={"head": src},
            device_id_type=MESH,
        ).wait_recv()
        hidden = hidden + mm(feat_in[src].reshape(users * share, cols), rank[src])
    second = r2[...].astype(F32)
    acted = silu(hidden)
    summed = acted[:, 0:128] * second[0:1, :]
    for i in range(1, second.shape[0]):
        summed = summed + acted[:, i * 128 : (i + 1) * 128] * second[i : i + 1, :]
    score_o[...] = jnp.sum(summed.reshape(users, share, 128), axis=-1)

    for cp in t_copies + rank_copies:
        cp.wait_send()
    for k in range(1, n_head):
        feat_copy(k).wait_send()
    if n_ctx > 1:

        @pl.when(me < last)
        def _():
            for p in range(pairs):
                right_copy(p).wait_send()

        @pl.when(me > 0)
        def _():
            for p in range(pairs):
                left_copy(p).wait_send()

    for cp in out_copies:
        cp.wait()


def results(hist_i, score_i, hist_o, score_o, sem):
    copies = [
        pltpu.make_async_copy(score_i, score_o, sem.at[0]),
    ]
    users = hist_i.shape[0]
    for u in range(users):
        copies.append(pltpu.make_async_copy(hist_i.at[u], hist_o.at[u], sem.at[u + 1]))
    for cp in copies:
        cp.start()
    for cp in copies:
        cp.wait()


def local(
    n_ctx,
    n_head,
    behavior_embed,
    behavior_mask,
    history_len,
    log_decay,
    candidate_embed,
    input_weight,
    input_gain,
    proj_weight,
    output_gain,
    ranker_first,
    ranker_second,
):
    users, span, embed = behavior_embed.shape
    cand = candidate_embed.shape[1]
    width, cols = proj_weight.shape[1:]
    hidden = ranker_first.shape[1]
    heads = cols // DH
    pairs = heads * users
    chunk = 256 if span % 256 == 0 else 128
    chunks = span // chunk
    share = cand // n_head
    wire = BF16 if n_ctx <= 8 else F32
    rows = users * span
    dma = pltpu.SemaphoreType.DMA
    hbm_spec = pl.BlockSpec(memory_space=pltpu.HBM)
    vmem_spec = pl.BlockSpec(memory_space=pltpu.VMEM)
    flops = 2 * rows * width * (embed + 4 * cols)
    history_out, scores = pl.pallas_call(
        functools.partial(kernel, n_ctx, n_head, chunk),
        out_shape=(
            jax.ShapeDtypeStruct((users, span, cols), BF16),
            jax.ShapeDtypeStruct((users, share), F32),
        ),
        in_specs=[pl.BlockSpec(memory_space=pltpu.SMEM)] + [hbm_spec] * 10,
        out_specs=(hbm_spec, vmem_spec),
        scratch_shapes=[
            pltpu.VMEM((users, span, embed), BF16),
            pltpu.VMEM((users, span), jnp.int32),
            pltpu.VMEM((heads, users, span), F32),
            pltpu.VMEM((users, cand, embed), BF16),
            pltpu.VMEM((embed, width), BF16),
            pltpu.VMEM((1, width), F32),
            pltpu.VMEM((4, width, cols), BF16),
            pltpu.VMEM((1, cols), F32),
            pltpu.VMEM((hidden // 128, 128), BF16),
            pltpu.VMEM((n_head, cols, hidden), BF16),
            pltpu.VMEM((rows, width), BF16),
            pltpu.VMEM((users * cand, width), BF16),
            pltpu.VMEM((rows, cols), BF16),
            pltpu.VMEM((rows, cols), BF16),
            pltpu.VMEM((rows, cols), BF16),
            pltpu.VMEM((rows, cols), F32),
            pltpu.VMEM((rows, cols), F32),
            pltpu.VMEM((users, span, cols), BF16),
            pltpu.VMEM((24, span), F32),
            pltpu.VMEM((pairs, chunks, DH, DH), F32),
            pltpu.VMEM((pairs, DH, DH), F32),
            pltpu.VMEM((n_ctx, 8, 128), F32),
            pltpu.VMEM((pairs, DH, DH), wire),
            pltpu.VMEM((pairs, DH, DH), wire),
            pltpu.VMEM((pairs, DH, DH), wire),
            pltpu.VMEM((pairs, DH, DH), wire),
            pltpu.VMEM((users, cand, cols), BF16),
            pltpu.VMEM((n_head, users, share, cols), BF16),
            dma((13,)),
            dma((users,)),
            dma((n_ctx,)),
            dma((n_ctx,)),
            dma((pairs,)),
            dma((pairs,)),
            dma((pairs,)),
            dma((pairs,)),
            dma((2 * n_head,)),
            dma((n_head,)),
            dma((n_head,)),
            dma((n_head,)),
        ],
        compiler_params=pltpu.CompilerParams(
            collective_id=0, has_side_effects=True, vmem_limit_bytes=60 * 1024 * 1024
        ),
        cost_estimate=pl.CostEstimate(
            flops=flops, bytes_accessed=6 * 1024 * 1024, transcendentals=0
        ),
    )(
        history_len,
        behavior_embed,
        behavior_mask,
        log_decay,
        candidate_embed,
        input_weight,
        input_gain.reshape(1, width),
        proj_weight,
        output_gain.reshape(1, cols),
        ranker_first,
        ranker_second.reshape(hidden // 128, 128),
    )
    return pl.pallas_call(
        results,
        out_shape=(
            jax.ShapeDtypeStruct(history_out.shape, BF16),
            jax.ShapeDtypeStruct(scores.shape, F32),
        ),
        in_specs=[hbm_spec, hbm_spec],
        out_specs=(hbm_spec, hbm_spec),
        scratch_shapes=[dma((users + 1,))],
        compiler_params=pltpu.CompilerParams(vmem_limit_bytes=60 * 1024 * 1024),
        cost_estimate=pl.CostEstimate(flops=0, bytes_accessed=1024 * 1024, transcendentals=0),
    )(history_out, scores)


def solution(mesh):
    in_specs = (
        P("grp", "ctx", None),
        P("grp", "ctx"),
        P("grp"),
        P("head", "grp", "ctx"),
        P("grp", "ctx", None),
        P(),
        P(),
        P(None, None, "head"),
        P("head"),
        P("head", None),
        P(),
    )
    out_specs = (P("grp", "ctx", "head"), P("grp", ("ctx", "head")))
    return jax.shard_map(
        functools.partial(local, mesh.shape["ctx"], mesh.shape["head"]),
        mesh=mesh,
        in_specs=in_specs,
        out_specs=out_specs,
        check_vma=False,
    )
```

```python
import functools

import jax
import jax.numpy as jnp
from jax import lax
from jax.experimental import pallas as pl
from jax.experimental.pallas import tpu as pltpu
from jax.sharding import PartitionSpec as P

DH = 128
CORES = 2
EPS = 1e-05
F32 = jnp.float32
BF16 = jnp.bfloat16
MESH = pl.DeviceIdType.MESH


def mm(a, b):
    return jnp.dot(a, b, preferred_element_type=F32)


def mm_tn(a, b):
    return lax.dot_general(a, b, (((0,), (0,)), ((), ())), preferred_element_type=F32)


def mm_nt(a, b):
    return lax.dot_general(a, b, (((1,), (1,)), ((), ())), preferred_element_type=F32)


def silu(x):
    return x / (1.0 + jnp.exp(-x))


def normed(rows, weight, gain):
    raw = mm(rows, weight).astype(BF16).astype(F32)
    scale = lax.rsqrt(jnp.mean(raw * raw, axis=-1, keepdims=True) + EPS)
    return (raw * scale * gain).astype(BF16)


def kernel(
    n_ctx,
    n_head,
    chunk,
    hl,
    be_h,
    mk_h,
    ld_h,
    ce_h,
    iw_h,
    ig_h,
    pw_h,
    og_h,
    rf_h,
    r2_h,
    hist,
    score_o,
    be,
    mk,
    ld,
    ce,
    iw,
    ig,
    pw,
    og,
    r2,
    rank,
    norm_s,
    cnorm,
    key_s,
    val_s,
    qry_s,
    gate_s,
    within_s,
    dat,
    lst,
    loc,
    tall,
    p_in,
    p_out,
    x_in,
    x_out,
    feat,
    feat_in,
    load_sem,
    t_send,
    t_recv,
    p_send,
    p_recv,
    x_send,
    x_recv,
    r_send,
    r_recv,
    f_send,
    f_recv,
):
    users, span, _ = be.shape
    cand = ce.shape[1]
    cols = og.shape[1]
    heads = cols // DH
    pairs = heads * users
    chunks = span // chunk
    share = cand // n_head
    me = lax.axis_index("ctx")
    hm = lax.axis_index("head")
    core = lax.rem(hm, CORES)

    loads = {}
    for i, (name, src, dst) in enumerate(
        (
            ("be", be_h, be),
            ("iw", iw_h, iw),
            ("ig", ig_h, ig),
            ("ld", ld_h, ld),
            ("mk", mk_h, mk),
            ("k", pw_h.at[1], pw.at[1]),
            ("v", pw_h.at[2], pw.at[2]),
            ("q", pw_h.at[0], pw.at[0]),
            ("g", pw_h.at[3], pw.at[3]),
            ("og", og_h, og),
            ("ce", ce_h, ce),
            ("r2", r2_h, r2),
            ("rf", rf_h, rank.at[hm]),
        )
    ):
        loads[name] = pltpu.make_async_copy(src, dst, load_sem.at[i])
        loads[name].start()

    barrier = pltpu.get_barrier_semaphore()
    for k in range(1, n_ctx):
        pl.semaphore_signal(
            barrier, inc=1, device_id={"ctx": lax.rem(me + k, n_ctx)}, device_id_type=MESH
        )
    for k in range(1, n_head):
        pl.semaphore_signal(
            barrier, inc=1, device_id={"head": lax.rem(hm + k, n_head)}, device_id_type=MESH
        )

    pl.semaphore_wait(barrier, n_ctx + n_head - 2)

    def rank_copy(slot, target, sem, src=None):
        return pltpu.make_async_remote_copy(
            src_ref=rank.at[slot] if src is None else src,
            dst_ref=rank.at[slot],
            send_sem=r_send.at[sem],
            recv_sem=r_recv.at[slot],
            device_id={"head": target},
            device_id_type=MESH,
        )

    sibling = hm + 1 - 2 * core
    rank_copies = []
    for k in range(CORES, n_head, CORES):
        rank_copies.append(rank_copy(hm, lax.rem(hm + k, n_head), k, rf_h))
        rank_copies[-1].start()
    rank_copies.append(rank_copy(hm, sibling, 0, rf_h))
    rank_copies[-1].start()

    for name in ("ld", "mk", "be", "iw", "ig", "k", "v"):
        loads[name].wait()
    dat[...] = jnp.zeros_like(dat)
    for u in range(users):
        for h in range(heads):
            p = u * heads + h
            dat[p : p + 1, :] = ld[h, u : u + 1, :]
    cum = dat[0:8, :]
    lane = lax.broadcasted_iota(jnp.int32, (8, span), 1)
    in_chunk = lax.rem(lane, chunk)
    step = 1
    while step < chunk:
        cum = cum + jnp.where(in_chunk >= step, pltpu.roll(cum, step, 1), 0.0)
        step *= 2
    ends = [cum[:, (c + 1) * chunk - 1 : (c + 1) * chunk] for c in range(chunks)]
    fades = [jnp.exp(e) for e in ends]
    end_total = functools.reduce(jnp.add, ends)
    fade_total = jnp.exp(end_total)
    end_row = ends[-1]
    for c in range(chunks - 2, -1, -1):
        end_row = jnp.where(lane < (c + 1) * chunk, ends[c], end_row)
    weight_rows = jnp.exp(end_row - cum)
    dat[0:8, :] = cum
    dat[8:16, :] = weight_rows
    dat[16:24, :] = jnp.exp(cum)
    pos = me * span + lax.broadcasted_iota(jnp.int32, (1, span), 1)
    valid = []
    for u in range(users):
        keep = (pos >= n_ctx * span - hl[u]) & (mk[u : u + 1, :] == 1)
        valid.append(jnp.where(keep, 1.0, 0.0))
    for h in range(heads):
        for u in range(users):
            p = 8 + u * heads + h
            dat[p : p + 1, :] = dat[p : p + 1, :] * valid[u]
    col = jnp.transpose(dat[...])
    tall[me] = jnp.broadcast_to(end_total, (8, 128))

    def right_copy(p):
        return pltpu.make_async_remote_copy(
            src_ref=p_out.at[p],
            dst_ref=p_in.at[p],
            send_sem=p_send.at[p],
            recv_sem=p_recv.at[p],
            device_id={"ctx": lax.rem(me + 1, n_ctx)},
            device_id_type=MESH,
        )

    def left_copy(p):
        return pltpu.make_async_remote_copy(
            src_ref=x_out.at[p],
            dst_ref=x_in.at[p],
            send_sem=x_send.at[p],
            recv_sem=x_recv.at[p],
            device_id={"ctx": lax.rem(me + n_ctx - 1, n_ctx)},
            device_id_type=MESH,
        )

    last = n_ctx - 1

    weight = iw[...]
    gain = ig[...]
    tri = lax.broadcasted_iota(jnp.int32, (chunk, chunk), 0) >= lax.broadcasted_iota(
        jnp.int32, (chunk, chunk), 1
    )

    def place(u, c):
        b = u * chunks + c
        return slice(b * chunk, (b + 1) * chunk), slice(c * chunk, (c + 1) * chunk)

    def keys_values(u, c):
        r, rc = place(u, c)
        rows = normed(be[u, rc, :], weight, gain)
        norm_s[r, :] = rows
        key = (mm(rows, pw[1]) * DH ** (-0.5)).astype(BF16)
        val = mm(rows, pw[2]).astype(BF16)
        key_s[r, :] = key
        val_s[r, :] = val
        for h in range(heads):
            p = u * heads + h
            hc = slice(h * DH, (h + 1) * DH)
            kw = (key[:, hc].astype(F32) * col[rc, 8 + p : 9 + p]).astype(BF16)
            lst[p, c] = mm_tn(kw, val[:, hc])

    def local_states(u):
        for p in range(u * heads, (u + 1) * heads):
            total = lst[p, 0]
            for c in range(1, chunks):
                total = total * fades[c][p : p + 1, :] + lst[p, c]
            loc[p] = total

    def first_sends(u):
        @pl.when(me == 0)
        def _():
            for p in range(u * heads, (u + 1) * heads):
                p_out[p] = loc[p].astype(p_out.dtype)
                if n_ctx > 1:
                    right_copy(p).start()

        @pl.when(me == last)
        def _():
            for p in range(u * heads, (u + 1) * heads):
                x_out[p] = loc[p].astype(x_out.dtype)
                if n_ctx > 1:
                    left_copy(p).start()

    def relay_right(u):
        for p in range(u * heads, (u + 1) * heads):
            right_copy(p).wait_recv()

            @pl.when(me < last)
            def _():
                p_out[p] = (
                    p_in[p].astype(F32) * fade_total[p : p + 1, :] + loc[p]
                ).astype(p_out.dtype)
                right_copy(p).start()

    def relay_left(u):
        for p in range(u * heads, (u + 1) * heads):
            left_copy(p).wait_recv()

            @pl.when(me > 0)
            def _():
                x_out[p] = (
                    x_in[p].astype(F32) + loc[p] * fade_after[p : p + 1, :]
                ).astype(x_out.dtype)
                left_copy(p).start()

    half = n_ctx // 2

    def near_relay(u):
        if n_ctx > 1:

            @pl.when((me > 0) & (me < half))
            def _():
                relay_right(u)

            @pl.when((me < last) & (me >= half))
            def _():
                relay_left(u)

    def far_relay(u, ends):
        if n_ctx > 1:
            at_end = (me == 0) | (me == last)
            turn = at_end if ends else jnp.logical_not(at_end)

            @pl.when(turn & (me < half))
            def _():
                relay_left(u)

            @pl.when(turn & (me >= half))
            def _():
                relay_right(u)

    def queries_gates(u):
        for c in range(chunks):
            r, _ = place(u, c)
            rows = norm_s[r, :]
            qry_s[r, :] = mm(rows, pw[0]).astype(BF16)
            gate_s[r, :] = silu(mm(rows, pw[3]).astype(BF16).astype(F32)) * out_gain

    def attention(u):
        for c in range(chunks):
            r, rc = place(u, c)
            seen = tri & (valid[u][:, rc] > 0.5)
            for h in range(heads):
                p = u * heads + h
                hc = slice(h * DH, (h + 1) * DH)
                gap = col[rc, p : p + 1] - dat[p : p + 1, rc]
                decay = jnp.where(seen, jnp.exp(jnp.where(tri, gap, 0.0)), 0.0)
                att = (mm_nt(qry_s[r, hc], key_s[r, hc]) * decay).astype(BF16)
                within_s[r, hc] = mm(att, val_s[r, hc])

    @pl.when(me == 0)
    def _():
        p_in[...] = jnp.zeros_like(p_in)

    @pl.when(me == last)
    def _():
        x_in[...] = jnp.zeros_like(x_in)

    t_copies = []
    for k in range(1, n_ctx):
        cp = pltpu.make_async_remote_copy(
            src_ref=tall.at[me],
            dst_ref=tall.at[me],
            send_sem=t_send.at[k],
            recv_sem=t_recv.at[me],
            device_id={"ctx": lax.rem(me + k, n_ctx)},
            device_id_type=MESH,
        )
        cp.start()
        t_copies.append(cp)

    for u in range(users):
        for c in range(chunks):
            keys_values(u, c)
        local_states(u)
        first_sends(u)

    for k in range(1, n_ctx):
        src = lax.rem(me + n_ctx - k, n_ctx)
        pltpu.make_async_remote_copy(
            src_ref=tall.at[src],
            dst_ref=tall.at[src],
            send_sem=t_send.at[k],
            recv_sem=t_recv.at[src],
            device_id={"ctx": lax.rem(me + k, n_ctx)},
            device_id_type=MESH,
        ).wait_recv()
    after = jnp.zeros((8, 128), F32)
    for j in range(n_ctx):
        after = after + jnp.where(j > me, tall[j], 0.0)
    fade_after = jnp.exp(after)[:, 0:1]

    for name in ("q", "g", "og", "ce", "r2", "rf"):
        loads[name].wait()
    out_gain = og[...]
    near_relay(0)
    for u in range(users):
        queries_gates(u)
        if u + 1 < users:
            near_relay(u + 1)
    far_relay(0, False)
    for u in range(users):
        attention(u)
        if u + 1 < users:
            far_relay(u + 1, False)
    cnorm[...] = normed(ce[...].reshape(users * cand, ce.shape[2]), weight, gain)
    cand_q = mm(cnorm[...], pw[0]).astype(BF16)
    own = cnorm[:, pl.ds(pl.multiple_of(hm * cols, DH), cols)].astype(F32)
    for u in range(users):
        far_relay(u, True)

    for p in range(pairs):
        u, h = p // heads, p % heads
        hc = slice(h * DH, (h + 1) * DH)
        rows = slice(u * cand, (u + 1) * cand)
        state = p_in[p].astype(F32) * fade_total[p : p + 1, :] + loc[p]
        state = state * fade_after[p : p + 1, :] + x_in[p].astype(F32)
        read = mm(cand_q[rows, hc], state.astype(BF16))
        scale = lax.rsqrt(jnp.mean(read * read, axis=-1, keepdims=True) + EPS)
        feat[u, :, hc] = (read * scale * out_gain[:, hc] + own[rows, hc]).astype(BF16)

    def feat_copy(k):
        target = lax.rem(hm + k, n_head)
        return pltpu.make_async_remote_copy(
            src_ref=feat.at[:, pl.ds(pl.multiple_of(target * share, share), share), :],
            dst_ref=feat_in.at[hm],
            send_sem=f_send.at[k],
            recv_sem=f_recv.at[hm],
            device_id={"head": target},
            device_id_type=MESH,
        )

    for k in range(1, n_head):
        feat_copy(k).start()

    for k in range(CORES, n_head, CORES):
        src = lax.rem(hm + n_head - k, n_head)
        rank_copy(src, sibling, k).wait_recv()
        rank_copies.append(rank_copy(src, sibling, n_head + k))
        rank_copies[-1].start()

    for u in range(users):
        for h in range(heads):
            p = u * heads + h
            hc = slice(h * DH, (h + 1) * DH)
            state = p_in[p].astype(F32)
            for c in range(chunks):
                r = slice((u * chunks + c) * chunk, (u * chunks + c + 1) * chunk)
                rc = slice(c * chunk, (c + 1) * chunk)
                read = within_s[r, hc] + col[rc, 16 + p : 17 + p] * mm(
                    qry_s[r, hc], state.astype(BF16)
                )
                scale = lax.rsqrt(jnp.mean(read * read, axis=-1, keepdims=True) + EPS)
                hist[u, rc, hc] = (read * scale * gate_s[r, hc]).astype(BF16)
                if c + 1 < chunks:
                    state = state * fades[c][p : p + 1, :] + lst[p, c]

    mine = feat[:, pl.ds(pl.multiple_of(hm * share, share), share), :]
    hidden = mm(mine.reshape(users * share, cols), rank[hm])
    rank_copy(sibling, sibling, 0).wait_recv()
    for k in range(CORES, n_head, CORES):
        src = lax.rem(sibling + n_head - k, n_head)
        rank_copy(src, sibling, n_head + k).wait_recv()
    for k in range(1, n_head):
        src = lax.rem(hm + n_head - k, n_head)
        pltpu.make_async_remote_copy(
            src_ref=feat_in.at[src],
            dst_ref=feat_in.at[src],
            send_sem=f_send.at[k],
            recv_sem=f_recv.at[src],
            device_id={"head": src},
            device_id_type=MESH,
        ).wait_recv()
        hidden = hidden + mm(feat_in[src].reshape(users * share, cols), rank[src])
    second = r2[...].astype(F32)
    acted = silu(hidden)
    summed = acted[:, 0:128] * second[0:1, :]
    for i in range(1, second.shape[0]):
        summed = summed + acted[:, i * 128 : (i + 1) * 128] * second[i : i + 1, :]
    score_o[...] = jnp.sum(summed.reshape(users, share, 128), axis=-1)

    for cp in t_copies + rank_copies:
        cp.wait_send()
    for k in range(1, n_head):
        feat_copy(k).wait_send()
    if n_ctx > 1:

        @pl.when(me < last)
        def _():
            for p in range(pairs):
                right_copy(p).wait_send()

        @pl.when(me > 0)
        def _():
            for p in range(pairs):
                left_copy(p).wait_send()


def results(hist_i, score_i, hist_o, score_o, sem):
    copies = [
        pltpu.make_async_copy(score_i, score_o, sem.at[0]),
    ]
    users = hist_i.shape[0]
    for u in range(users):
        copies.append(pltpu.make_async_copy(hist_i.at[u], hist_o.at[u], sem.at[u + 1]))
    for cp in copies:
        cp.start()
    for cp in copies:
        cp.wait()


def local(
    n_ctx,
    n_head,
    behavior_embed,
    behavior_mask,
    history_len,
    log_decay,
    candidate_embed,
    input_weight,
    input_gain,
    proj_weight,
    output_gain,
    ranker_first,
    ranker_second,
):
    users, span, embed = behavior_embed.shape
    cand = candidate_embed.shape[1]
    width, cols = proj_weight.shape[1:]
    hidden = ranker_first.shape[1]
    heads = cols // DH
    pairs = heads * users
    chunk = 256 if span % 256 == 0 else 128
    chunks = span // chunk
    share = cand // n_head
    wire = BF16 if n_ctx <= 8 else F32
    rows = users * span
    dma = pltpu.SemaphoreType.DMA
    hbm_spec = pl.BlockSpec(memory_space=pltpu.HBM)
    vmem_spec = pl.BlockSpec(memory_space=pltpu.VMEM)
    flops = 2 * rows * width * (embed + 4 * cols)
    history_out, scores = pl.pallas_call(
        functools.partial(kernel, n_ctx, n_head, chunk),
        out_shape=(
            pltpu.VMEM((users, span, cols), BF16),
            pltpu.VMEM((users, share), F32),
        ),
        in_specs=[pl.BlockSpec(memory_space=pltpu.SMEM)] + [hbm_spec] * 10,
        out_specs=(vmem_spec, vmem_spec),
        scratch_shapes=[
            pltpu.VMEM((users, span, embed), BF16),
            pltpu.VMEM((users, span), jnp.int32),
            pltpu.VMEM((heads, users, span), F32),
            pltpu.VMEM((users, cand, embed), BF16),
            pltpu.VMEM((embed, width), BF16),
            pltpu.VMEM((1, width), F32),
            pltpu.VMEM((4, width, cols), BF16),
            pltpu.VMEM((1, cols), F32),
            pltpu.VMEM((hidden // 128, 128), BF16),
            pltpu.VMEM((n_head, cols, hidden), BF16),
            pltpu.VMEM((rows, width), BF16),
            pltpu.VMEM((users * cand, width), BF16),
            pltpu.VMEM((rows, cols), BF16),
            pltpu.VMEM((rows, cols), BF16),
            pltpu.VMEM((rows, cols), BF16),
            pltpu.VMEM((rows, cols), F32),
            pltpu.VMEM((rows, cols), F32),
            pltpu.VMEM((24, span), F32),
            pltpu.VMEM((pairs, chunks, DH, DH), F32),
            pltpu.VMEM((pairs, DH, DH), F32),
            pltpu.VMEM((n_ctx, 8, 128), F32),
            pltpu.VMEM((pairs, DH, DH), wire),
            pltpu.VMEM((pairs, DH, DH), wire),
            pltpu.VMEM((pairs, DH, DH), wire),
            pltpu.VMEM((pairs, DH, DH), wire),
            pltpu.VMEM((users, cand, cols), BF16),
            pltpu.VMEM((n_head, users, share, cols), BF16),
            dma((13,)),
            dma((n_ctx,)),
            dma((n_ctx,)),
            dma((pairs,)),
            dma((pairs,)),
            dma((pairs,)),
            dma((pairs,)),
            dma((2 * n_head,)),
            dma((n_head,)),
            dma((n_head,)),
            dma((n_head,)),
        ],
        compiler_params=pltpu.CompilerParams(
            collective_id=0, has_side_effects=True, vmem_limit_bytes=60 * 1024 * 1024
        ),
        cost_estimate=pl.CostEstimate(
            flops=flops, bytes_accessed=6 * 1024 * 1024, transcendentals=0
        ),
    )(
        history_len,
        behavior_embed,
        behavior_mask,
        log_decay,
        candidate_embed,
        input_weight,
        input_gain.reshape(1, width),
        proj_weight,
        output_gain.reshape(1, cols),
        ranker_first,
        ranker_second.reshape(hidden // 128, 128),
    )
    return pl.pallas_call(
        results,
        out_shape=(
            jax.ShapeDtypeStruct(history_out.shape, BF16),
            jax.ShapeDtypeStruct(scores.shape, F32),
        ),
        in_specs=[vmem_spec, vmem_spec],
        out_specs=(hbm_spec, hbm_spec),
        scratch_shapes=[dma((users + 1,))],
        compiler_params=pltpu.CompilerParams(vmem_limit_bytes=8 * 1024 * 1024),
        cost_estimate=pl.CostEstimate(flops=0, bytes_accessed=1024 * 1024, transcendentals=0),
    )(history_out, scores)


def solution(mesh):
    in_specs = (
        P("grp", "ctx", None),
        P("grp", "ctx"),
        P("grp"),
        P("head", "grp", "ctx"),
        P("grp", "ctx", None),
        P(),
        P(),
        P(None, None, "head"),
        P("head"),
        P("head", None),
        P(),
    )
    out_specs = (P("grp", "ctx", "head"), P("grp", ("ctx", "head")))
    return jax.shard_map(
        functools.partial(local, mesh.shape["ctx"], mesh.shape["head"]),
        mesh=mesh,
        in_specs=in_specs,
        out_specs=out_specs,
        check_vma=False,
    )
```

```python
import functools

import jax
import jax.numpy as jnp
from jax import lax
from jax.experimental import pallas as pl
from jax.experimental.pallas import tpu as pltpu
from jax.sharding import PartitionSpec as P

DH = 128
CORES = 2
EPS = 1e-05
F32 = jnp.float32
BF16 = jnp.bfloat16
MESH = pl.DeviceIdType.MESH


def mm(a, b):
    return jnp.dot(a, b, preferred_element_type=F32)


def mm_tn(a, b):
    return lax.dot_general(a, b, (((0,), (0,)), ((), ())), preferred_element_type=F32)


def mm_nt(a, b):
    return lax.dot_general(a, b, (((1,), (1,)), ((), ())), preferred_element_type=F32)


def silu(x):
    return x / (1.0 + jnp.exp(-x))


def normed(rows, weight, gain):
    raw = mm(rows, weight).astype(BF16).astype(F32)
    scale = lax.rsqrt(jnp.mean(raw * raw, axis=-1, keepdims=True) + EPS)
    return (raw * scale * gain).astype(BF16)


def kernel(
    n_ctx,
    n_head,
    chunk,
    hl,
    be_h,
    mk_h,
    ld_h,
    ce_h,
    iw_h,
    ig_h,
    pw_h,
    og_h,
    rf_h,
    r2_h,
    hist,
    score_o,
    be,
    mk,
    ld,
    ce,
    iw,
    ig,
    pw,
    og,
    r2,
    rank,
    norm_s,
    cnorm,
    key_s,
    val_s,
    qry_s,
    gate_s,
    within_s,
    dat,
    lst,
    loc,
    tall,
    p_in,
    p_out,
    x_in,
    x_out,
    feat,
    feat_in,
    load_sem,
    t_send,
    t_recv,
    p_send,
    p_recv,
    x_send,
    x_recv,
    r_send,
    r_recv,
    f_send,
    f_recv,
):
    users, span, _ = be.shape
    cand = ce.shape[1]
    cols = og.shape[1]
    heads = cols // DH
    pairs = heads * users
    chunks = span // chunk
    share = cand // n_head
    me = lax.axis_index("ctx")
    hm = lax.axis_index("head")
    core = lax.rem(hm, CORES)

    loads = {}
    for i, (name, src, dst) in enumerate(
        (
            ("be", be_h, be),
            ("iw", iw_h, iw),
            ("ig", ig_h, ig),
            ("ld", ld_h, ld),
            ("mk", mk_h, mk),
            ("k", pw_h.at[1], pw.at[1]),
            ("v", pw_h.at[2], pw.at[2]),
            ("q", pw_h.at[0], pw.at[0]),
            ("g", pw_h.at[3], pw.at[3]),
            ("og", og_h, og),
            ("ce", ce_h, ce),
            ("r2", r2_h, r2),
            ("rf", rf_h, rank.at[hm]),
        )
    ):
        loads[name] = pltpu.make_async_copy(src, dst, load_sem.at[i])
        loads[name].start()

    barrier = pltpu.get_barrier_semaphore()
    for k in range(1, n_ctx):
        pl.semaphore_signal(
            barrier, inc=1, device_id={"ctx": lax.rem(me + k, n_ctx)}, device_id_type=MESH
        )
    for k in range(1, n_head):
        pl.semaphore_signal(
            barrier, inc=1, device_id={"head": lax.rem(hm + k, n_head)}, device_id_type=MESH
        )

    pl.semaphore_wait(barrier, n_ctx + n_head - 2)

    def rank_copy(slot, target, sem, src=None):
        return pltpu.make_async_remote_copy(
            src_ref=rank.at[slot] if src is None else src,
            dst_ref=rank.at[slot],
            send_sem=r_send.at[sem],
            recv_sem=r_recv.at[slot],
            device_id={"head": target},
            device_id_type=MESH,
        )

    sibling = hm + 1 - 2 * core
    rank_copies = []
    for k in range(CORES, n_head, CORES):
        rank_copies.append(rank_copy(hm, lax.rem(hm + k, n_head), k, rf_h))
        rank_copies[-1].start()
    rank_copies.append(rank_copy(hm, sibling, 0, rf_h))
    rank_copies[-1].start()

    for name in ("ld", "mk", "be", "iw", "ig", "k", "v"):
        loads[name].wait()
    dat[...] = jnp.zeros_like(dat)
    for u in range(users):
        for h in range(heads):
            p = u * heads + h
            dat[p : p + 1, :] = ld[h, u : u + 1, :]
    cum = dat[0:8, :]
    lane = lax.broadcasted_iota(jnp.int32, (8, span), 1)
    in_chunk = lax.rem(lane, chunk)
    step = 1
    while step < chunk:
        cum = cum + jnp.where(in_chunk >= step, pltpu.roll(cum, step, 1), 0.0)
        step *= 2
    ends = [cum[:, (c + 1) * chunk - 1 : (c + 1) * chunk] for c in range(chunks)]
    fades = [jnp.exp(e) for e in ends]
    end_total = functools.reduce(jnp.add, ends)
    fade_total = jnp.exp(end_total)
    end_row = ends[-1]
    for c in range(chunks - 2, -1, -1):
        end_row = jnp.where(lane < (c + 1) * chunk, ends[c], end_row)
    weight_rows = jnp.exp(end_row - cum)
    dat[0:8, :] = cum
    dat[8:16, :] = weight_rows
    dat[16:24, :] = jnp.exp(cum)
    pos = me * span + lax.broadcasted_iota(jnp.int32, (1, span), 1)
    valid = []
    for u in range(users):
        keep = (pos >= n_ctx * span - hl[u]) & (mk[u : u + 1, :] == 1)
        valid.append(jnp.where(keep, 1.0, 0.0))
    for h in range(heads):
        for u in range(users):
            p = 8 + u * heads + h
            dat[p : p + 1, :] = dat[p : p + 1, :] * valid[u]
    col = jnp.transpose(dat[...])
    tall[me] = jnp.broadcast_to(end_total, (8, 128))

    def right_copy(p):
        return pltpu.make_async_remote_copy(
            src_ref=p_out.at[p],
            dst_ref=p_in.at[p],
            send_sem=p_send.at[p],
            recv_sem=p_recv.at[p],
            device_id={"ctx": lax.rem(me + 1, n_ctx)},
            device_id_type=MESH,
        )

    def left_copy(p):
        return pltpu.make_async_remote_copy(
            src_ref=x_out.at[p],
            dst_ref=x_in.at[p],
            send_sem=x_send.at[p],
            recv_sem=x_recv.at[p],
            device_id={"ctx": lax.rem(me + n_ctx - 1, n_ctx)},
            device_id_type=MESH,
        )

    last = n_ctx - 1

    weight = iw[...]
    gain = ig[...]
    tri = lax.broadcasted_iota(jnp.int32, (chunk, chunk), 0) >= lax.broadcasted_iota(
        jnp.int32, (chunk, chunk), 1
    )

    def place(u, c):
        b = u * chunks + c
        return slice(b * chunk, (b + 1) * chunk), slice(c * chunk, (c + 1) * chunk)

    def keys_values(u):
        ru = slice(u * span, (u + 1) * span)
        rows = normed(be[u], weight, gain)
        norm_s[ru, :] = rows
        key_s[ru, :] = (mm(rows, pw[1]) * DH ** (-0.5)).astype(BF16)
        val_s[ru, :] = mm(rows, pw[2]).astype(BF16)
        for h in range(heads):
            p = u * heads + h
            hc = slice(h * DH, (h + 1) * DH)
            for c in range(chunks):
                r, rc = place(u, c)
                kw = (key_s[r, hc].astype(F32) * col[rc, 8 + p : 9 + p]).astype(BF16)
                lst[p, c] = mm_tn(kw, val_s[r, hc])

    def local_states(u):
        for p in range(u * heads, (u + 1) * heads):
            total = lst[p, 0]
            for c in range(1, chunks):
                total = total * fades[c][p : p + 1, :] + lst[p, c]
            loc[p] = total

    def first_sends(u):
        @pl.when(me == 0)
        def _():
            for p in range(u * heads, (u + 1) * heads):
                p_out[p] = loc[p].astype(p_out.dtype)
                if n_ctx > 1:
                    right_copy(p).start()

        @pl.when(me == last)
        def _():
            for p in range(u * heads, (u + 1) * heads):
                x_out[p] = loc[p].astype(x_out.dtype)
                if n_ctx > 1:
                    left_copy(p).start()

    def relay_right(u):
        for p in range(u * heads, (u + 1) * heads):
            right_copy(p).wait_recv()

            @pl.when(me < last)
            def _():
                p_out[p] = (
                    p_in[p].astype(F32) * fade_total[p : p + 1, :] + loc[p]
                ).astype(p_out.dtype)
                right_copy(p).start()

    def relay_left(u):
        for p in range(u * heads, (u + 1) * heads):
            left_copy(p).wait_recv()

            @pl.when(me > 0)
            def _():
                x_out[p] = (
                    x_in[p].astype(F32) + loc[p] * fade_after[p : p + 1, :]
                ).astype(x_out.dtype)
                left_copy(p).start()

    half = n_ctx // 2

    def near_relay(u):
        if n_ctx > 1:

            @pl.when((me > 0) & (me < half))
            def _():
                relay_right(u)

            @pl.when((me < last) & (me >= half))
            def _():
                relay_left(u)

    def far_relay(u, ends):
        if n_ctx > 1:
            at_end = (me == 0) | (me == last)
            turn = at_end if ends else jnp.logical_not(at_end)

            @pl.when(turn & (me < half))
            def _():
                relay_left(u)

            @pl.when(turn & (me >= half))
            def _():
                relay_right(u)

    def queries_gates(u):
        ru = slice(u * span, (u + 1) * span)
        rows = norm_s[ru, :]
        qry_s[ru, :] = mm(rows, pw[0]).astype(BF16)
        gate_s[ru, :] = silu(mm(rows, pw[3]).astype(BF16).astype(F32)) * out_gain

    def attention(u):
        for c in range(chunks):
            r, rc = place(u, c)
            seen = tri & (valid[u][:, rc] > 0.5)
            for h in range(heads):
                p = u * heads + h
                hc = slice(h * DH, (h + 1) * DH)
                gap = col[rc, p : p + 1] - dat[p : p + 1, rc]
                decay = jnp.where(seen, jnp.exp(jnp.where(tri, gap, 0.0)), 0.0)
                att = (mm_nt(qry_s[r, hc], key_s[r, hc]) * decay).astype(BF16)
                within_s[r, hc] = mm(att, val_s[r, hc])

    @pl.when(me == 0)
    def _():
        p_in[...] = jnp.zeros_like(p_in)

    @pl.when(me == last)
    def _():
        x_in[...] = jnp.zeros_like(x_in)

    t_copies = []
    for k in range(1, n_ctx):
        cp = pltpu.make_async_remote_copy(
            src_ref=tall.at[me],
            dst_ref=tall.at[me],
            send_sem=t_send.at[k],
            recv_sem=t_recv.at[me],
            device_id={"ctx": lax.rem(me + k, n_ctx)},
            device_id_type=MESH,
        )
        cp.start()
        t_copies.append(cp)

    for u in range(users):
        keys_values(u)
        local_states(u)
        first_sends(u)

    for k in range(1, n_ctx):
        src = lax.rem(me + n_ctx - k, n_ctx)
        pltpu.make_async_remote_copy(
            src_ref=tall.at[src],
            dst_ref=tall.at[src],
            send_sem=t_send.at[k],
            recv_sem=t_recv.at[src],
            device_id={"ctx": lax.rem(me + k, n_ctx)},
            device_id_type=MESH,
        ).wait_recv()
    after = jnp.zeros((8, 128), F32)
    for j in range(n_ctx):
        after = after + jnp.where(j > me, tall[j], 0.0)
    fade_after = jnp.exp(after)[:, 0:1]

    for name in ("q", "g", "og", "ce", "r2", "rf"):
        loads[name].wait()
    out_gain = og[...]
    near_relay(0)
    for u in range(users):
        queries_gates(u)
    for u in range(1, users):
        near_relay(u)
    far_relay(0, False)
    attention(0)
    cnorm[...] = normed(ce[...].reshape(users * cand, ce.shape[2]), weight, gain)
    cand_q = mm(cnorm[...], pw[0]).astype(BF16)
    own = cnorm[:, pl.ds(pl.multiple_of(hm * cols, DH), cols)].astype(F32)
    for u in range(1, users):
        far_relay(u, False)

    def candidates(u):
        rows = slice(u * cand, (u + 1) * cand)
        for h in range(heads):
            p = u * heads + h
            hc = slice(h * DH, (h + 1) * DH)
            state = p_in[p].astype(F32) * fade_total[p : p + 1, :] + loc[p]
            state = state * fade_after[p : p + 1, :] + x_in[p].astype(F32)
            read = mm(cand_q[rows, hc], state.astype(BF16))
            scale = lax.rsqrt(jnp.mean(read * read, axis=-1, keepdims=True) + EPS)
            feat[u, :, hc] = (read * scale * out_gain[:, hc] + own[rows, hc]).astype(BF16)
        for k in range(1, n_head):
            feat_copy(u, k).start()

    def feat_copy(u, k):
        target = lax.rem(hm + k, n_head)
        return pltpu.make_async_remote_copy(
            src_ref=feat.at[u, pl.ds(pl.multiple_of(target * share, share), share), :],
            dst_ref=feat_in.at[hm, u],
            send_sem=f_send.at[u, k],
            recv_sem=f_recv.at[u, hm],
            device_id={"head": target},
            device_id_type=MESH,
        )

    def histories(u):
        for h in range(heads):
            p = u * heads + h
            hc = slice(h * DH, (h + 1) * DH)
            state = p_in[p].astype(F32)
            for c in range(chunks):
                r, rc = place(u, c)
                read = within_s[r, hc] + col[rc, 16 + p : 17 + p] * mm(
                    qry_s[r, hc], state.astype(BF16)
                )
                scale = lax.rsqrt(jnp.mean(read * read, axis=-1, keepdims=True) + EPS)
                hist[u, rc, hc] = (read * scale * gate_s[r, hc]).astype(BF16)
                if c + 1 < chunks:
                    state = state * fades[c][p : p + 1, :] + lst[p, c]

    for u in range(users):
        far_relay(u, True)
        candidates(u)
        if u + 1 < users:
            attention(u + 1)
            histories(u)

    for k in range(CORES, n_head, CORES):
        src = lax.rem(hm + n_head - k, n_head)
        rank_copy(src, sibling, k).wait_recv()
        rank_copies.append(rank_copy(src, sibling, n_head + k))
        rank_copies[-1].start()

    histories(users - 1)

    mine = feat[:, pl.ds(pl.multiple_of(hm * share, share), share), :]
    hidden = mm(mine.reshape(users * share, cols), rank[hm])
    rank_copy(sibling, sibling, 0).wait_recv()
    for k in range(CORES, n_head, CORES):
        src = lax.rem(sibling + n_head - k, n_head)
        rank_copy(src, sibling, n_head + k).wait_recv()
    for k in range(1, n_head):
        src = lax.rem(hm + n_head - k, n_head)
        for u in range(users):
            pltpu.make_async_remote_copy(
                src_ref=feat_in.at[src, u],
                dst_ref=feat_in.at[src, u],
                send_sem=f_send.at[u, k],
                recv_sem=f_recv.at[u, src],
                device_id={"head": src},
                device_id_type=MESH,
            ).wait_recv()
        hidden = hidden + mm(feat_in[src].reshape(users * share, cols), rank[src])
    second = r2[...].astype(F32)
    acted = silu(hidden)
    summed = acted[:, 0:128] * second[0:1, :]
    for i in range(1, second.shape[0]):
        summed = summed + acted[:, i * 128 : (i + 1) * 128] * second[i : i + 1, :]
    score_o[...] = jnp.sum(summed.reshape(users, share, 128), axis=-1)

    for cp in t_copies + rank_copies:
        cp.wait_send()
    for u in range(users):
        for k in range(1, n_head):
            feat_copy(u, k).wait_send()
    if n_ctx > 1:

        @pl.when(me < last)
        def _():
            for p in range(pairs):
                right_copy(p).wait_send()

        @pl.when(me > 0)
        def _():
            for p in range(pairs):
                left_copy(p).wait_send()


def results(hist_i, score_i, hist_o, score_o, sem):
    copies = [
        pltpu.make_async_copy(score_i, score_o, sem.at[0]),
    ]
    users = hist_i.shape[0]
    for u in range(users):
        copies.append(pltpu.make_async_copy(hist_i.at[u], hist_o.at[u], sem.at[u + 1]))
    for cp in copies:
        cp.start()
    for cp in copies:
        cp.wait()


def local(
    n_ctx,
    n_head,
    behavior_embed,
    behavior_mask,
    history_len,
    log_decay,
    candidate_embed,
    input_weight,
    input_gain,
    proj_weight,
    output_gain,
    ranker_first,
    ranker_second,
):
    users, span, embed = behavior_embed.shape
    cand = candidate_embed.shape[1]
    width, cols = proj_weight.shape[1:]
    hidden = ranker_first.shape[1]
    heads = cols // DH
    pairs = heads * users
    chunk = 256 if span % 256 == 0 else 128
    chunks = span // chunk
    share = cand // n_head
    wire = BF16 if n_ctx <= 8 else F32
    rows = users * span
    dma = pltpu.SemaphoreType.DMA
    hbm_spec = pl.BlockSpec(memory_space=pltpu.HBM)
    vmem_spec = pl.BlockSpec(memory_space=pltpu.VMEM)
    flops = 2 * rows * width * (embed + 4 * cols)
    history_out, scores = pl.pallas_call(
        functools.partial(kernel, n_ctx, n_head, chunk),
        out_shape=(
            pltpu.VMEM((users, span, cols), BF16),
            pltpu.VMEM((users, share), F32),
        ),
        in_specs=[pl.BlockSpec(memory_space=pltpu.SMEM)] + [hbm_spec] * 10,
        out_specs=(vmem_spec, vmem_spec),
        scratch_shapes=[
            pltpu.VMEM((users, span, embed), BF16),
            pltpu.VMEM((users, span), jnp.int32),
            pltpu.VMEM((heads, users, span), F32),
            pltpu.VMEM((users, cand, embed), BF16),
            pltpu.VMEM((embed, width), BF16),
            pltpu.VMEM((1, width), F32),
            pltpu.VMEM((4, width, cols), BF16),
            pltpu.VMEM((1, cols), F32),
            pltpu.VMEM((hidden // 128, 128), BF16),
            pltpu.VMEM((n_head, cols, hidden), BF16),
            pltpu.VMEM((rows, width), BF16),
            pltpu.VMEM((users * cand, width), BF16),
            pltpu.VMEM((rows, cols), BF16),
            pltpu.VMEM((rows, cols), BF16),
            pltpu.VMEM((rows, cols), BF16),
            pltpu.VMEM((rows, cols), F32),
            pltpu.VMEM((rows, cols), F32),
            pltpu.VMEM((24, span), F32),
            pltpu.VMEM((pairs, chunks, DH, DH), F32),
            pltpu.VMEM((pairs, DH, DH), F32),
            pltpu.VMEM((n_ctx, 8, 128), F32),
            pltpu.VMEM((pairs, DH, DH), wire),
            pltpu.VMEM((pairs, DH, DH), wire),
            pltpu.VMEM((pairs, DH, DH), wire),
            pltpu.VMEM((pairs, DH, DH), wire),
            pltpu.VMEM((users, cand, cols), BF16),
            pltpu.VMEM((n_head, users, share, cols), BF16),
            dma((13,)),
            dma((n_ctx,)),
            dma((n_ctx,)),
            dma((pairs,)),
            dma((pairs,)),
            dma((pairs,)),
            dma((pairs,)),
            dma((2 * n_head,)),
            dma((n_head,)),
            dma((users, n_head)),
            dma((users, n_head)),
        ],
        compiler_params=pltpu.CompilerParams(
            collective_id=0, has_side_effects=True, vmem_limit_bytes=60 * 1024 * 1024
        ),
        cost_estimate=pl.CostEstimate(
            flops=flops, bytes_accessed=6 * 1024 * 1024, transcendentals=0
        ),
    )(
        history_len,
        behavior_embed,
        behavior_mask,
        log_decay,
        candidate_embed,
        input_weight,
        input_gain.reshape(1, width),
        proj_weight,
        output_gain.reshape(1, cols),
        ranker_first,
        ranker_second.reshape(hidden // 128, 128),
    )
    return pl.pallas_call(
        results,
        out_shape=(
            jax.ShapeDtypeStruct(history_out.shape, BF16),
            jax.ShapeDtypeStruct(scores.shape, F32),
        ),
        in_specs=[vmem_spec, vmem_spec],
        out_specs=(hbm_spec, hbm_spec),
        scratch_shapes=[dma((users + 1,))],
        compiler_params=pltpu.CompilerParams(vmem_limit_bytes=8 * 1024 * 1024),
        cost_estimate=pl.CostEstimate(flops=0, bytes_accessed=1024 * 1024, transcendentals=0),
    )(history_out, scores)


def solution(mesh):
    in_specs = (
        P("grp", "ctx", None),
        P("grp", "ctx"),
        P("grp"),
        P("head", "grp", "ctx"),
        P("grp", "ctx", None),
        P(),
        P(),
        P(None, None, "head"),
        P("head"),
        P("head", None),
        P(),
    )
    out_specs = (P("grp", "ctx", "head"), P("grp", ("ctx", "head")))
    return jax.shard_map(
        functools.partial(local, mesh.shape["ctx"], mesh.shape["head"]),
        mesh=mesh,
        in_specs=in_specs,
        out_specs=out_specs,
        check_vma=False,
    )
```

```python
import functools

import jax
import jax.numpy as jnp
from jax import lax
from jax.experimental import pallas as pl
from jax.experimental.pallas import tpu as pltpu
from jax.sharding import PartitionSpec as P

DH = 128
CORES = 2
EPS = 1e-05
F32 = jnp.float32
BF16 = jnp.bfloat16
MESH = pl.DeviceIdType.MESH


def mm(a, b):
    return jnp.dot(a, b, preferred_element_type=F32)


def mm_tn(a, b):
    return lax.dot_general(a, b, (((0,), (0,)), ((), ())), preferred_element_type=F32)


def mm_nt(a, b):
    return lax.dot_general(a, b, (((1,), (1,)), ((), ())), preferred_element_type=F32)


def silu(x):
    return x / (1.0 + jnp.exp(-x))


def normed(rows, weight, gain):
    raw = mm(rows, weight).astype(BF16).astype(F32)
    scale = lax.rsqrt(jnp.mean(raw * raw, axis=-1, keepdims=True) + EPS)
    return (raw * scale * gain).astype(BF16)


def kernel(
    n_grp,
    n_ctx,
    n_head,
    chunk,
    hl,
    be_h,
    mk_h,
    ld_h,
    ce_h,
    iw_h,
    ig_h,
    pw_h,
    og_h,
    rf_h,
    r2_h,
    hist,
    score_o,
    be,
    mk,
    ld,
    ce,
    iw,
    ig,
    pw,
    og,
    r2,
    rank,
    norm_s,
    cnorm,
    key_s,
    val_s,
    qry_s,
    gate_s,
    within_s,
    dat,
    lst,
    loc,
    tall,
    p_in,
    p_out,
    x_in,
    x_out,
    feat,
    feat_in,
    load_sem,
    t_send,
    t_recv,
    p_send,
    p_recv,
    x_send,
    x_recv,
    r_send,
    r_recv,
    wx_send,
    wx_recv,
    wy_send,
    wy_recv,
    wf_send,
    wf_recv,
    f_send,
    f_recv,
):
    users, span, _ = be.shape
    cand = ce.shape[1]
    cols = og.shape[1]
    heads = cols // DH
    pairs = heads * users
    chunks = span // chunk
    share = cand // n_head
    me = lax.axis_index("ctx")
    hm = lax.axis_index("head")
    core = lax.rem(hm, CORES)

    loads = {}
    for i, (name, src, dst) in enumerate(
        (
            ("be", be_h, be),
            ("iw", iw_h, iw),
            ("ig", ig_h, ig),
            ("ld", ld_h, ld),
            ("mk", mk_h, mk),
            ("k", pw_h.at[1], pw.at[1]),
            ("v", pw_h.at[2], pw.at[2]),
            ("q", pw_h.at[0], pw.at[0]),
            ("g", pw_h.at[3], pw.at[3]),
            ("og", og_h, og),
            ("ce", ce_h, ce),
            ("r2", r2_h, r2),
            ("rf", rf_h, rank.at[hm]),
        )
    ):
        loads[name] = pltpu.make_async_copy(src, dst, load_sem.at[i])
        loads[name].start()

    barrier = pltpu.get_barrier_semaphore()
    for k in range(1, n_ctx):
        pl.semaphore_signal(
            barrier, inc=1, device_id={"ctx": lax.rem(me + k, n_ctx)}, device_id_type=MESH
        )
    for k in range(1, n_head):
        pl.semaphore_signal(
            barrier, inc=1, device_id={"head": lax.rem(hm + k, n_head)}, device_id_type=MESH
        )

    paired = n_grp == 2
    if paired:
        pl.semaphore_signal(
            barrier, inc=1, device_id={"grp": 1 - lax.axis_index("grp")}, device_id_type=MESH
        )
    pl.semaphore_wait(barrier, n_ctx + n_head - 2 + int(paired))

    def rank_copy(slot, target, sem, src=None):
        return pltpu.make_async_remote_copy(
            src_ref=rank.at[slot] if src is None else src,
            dst_ref=rank.at[slot],
            send_sem=r_send.at[sem],
            recv_sem=r_recv.at[slot],
            device_id={"head": target},
            device_id_type=MESH,
        )

    sibling = hm + 1 - 2 * core
    rank_copies = []
    mine_g = lax.axis_index("grp") if paired else 0
    other_g = 1 - mine_g
    nx, ny = (5, 3) if paired else (8, 0)
    depth = cols // 8

    def piece(slot, s, grp, target, send, recv, src=None):
        rows = pl.ds(pl.multiple_of((s + grp * (7 - 2 * s)) * depth, depth), depth)
        return pltpu.make_async_remote_copy(
            src_ref=rank.at[slot, rows, :] if src is None else src.at[rows, :],
            dst_ref=rank.at[slot, rows, :],
            send_sem=send,
            recv_sem=recv,
            device_id=target,
            device_id_type=MESH,
        )

    def along_x(slot, target, k, s, src=None):
        return piece(
            slot, s, mine_g, {"head": target}, wx_send.at[k, s], wx_recv.at[slot, s], src
        )

    def along_y(slot, k, s, grp):
        return piece(slot, s, grp, {"grp": other_g}, wy_send.at[k, s], wy_recv.at[slot, s])

    def to_sibling(slot, k, s, grp, i):
        return piece(slot, s, grp, {"head": sibling}, wf_send.at[k, i], wf_recv.at[slot, i])

    def pass_on(steps):
        for s in steps:
            for k in range(CORES, n_head, CORES):
                slot = lax.rem(hm + n_head - k, n_head)
                along_x(slot, slot, k, s).wait_recv()
                if s < ny:
                    rank_copies.append(along_y(slot, k, s, mine_g))
                    rank_copies[-1].start()
                rank_copies.append(to_sibling(slot, k, s, mine_g, s))
                rank_copies[-1].start()

    def pass_on_y(steps):
        for s in steps:
            for k in range(CORES, n_head, CORES):
                slot = lax.rem(hm + n_head - k, n_head)
                along_y(slot, k, s, other_g).wait_recv()
                rank_copies.append(to_sibling(slot, k, s, other_g, nx + s))
                rank_copies[-1].start()

    for s in range(nx):
        for k in range(CORES, n_head, CORES):
            rank_copies.append(along_x(hm, lax.rem(hm + k, n_head), k, s, rf_h))
            rank_copies[-1].start()
    rank_copies.append(rank_copy(hm, sibling, 0, rf_h))
    rank_copies[-1].start()

    for name in ("ld", "mk", "be", "iw", "ig", "k", "v"):
        loads[name].wait()
    dat[...] = jnp.zeros_like(dat)
    for u in range(users):
        for h in range(heads):
            p = u * heads + h
            dat[p : p + 1, :] = ld[h, u : u + 1, :]
    cum = dat[0:8, :]
    lane = lax.broadcasted_iota(jnp.int32, (8, span), 1)
    in_chunk = lax.rem(lane, chunk)
    step = 1
    while step < chunk:
        cum = cum + jnp.where(in_chunk >= step, pltpu.roll(cum, step, 1), 0.0)
        step *= 2
    ends = [cum[:, (c + 1) * chunk - 1 : (c + 1) * chunk] for c in range(chunks)]
    fades = [jnp.exp(e) for e in ends]
    end_total = functools.reduce(jnp.add, ends)
    fade_total = jnp.exp(end_total)
    end_row = ends[-1]
    for c in range(chunks - 2, -1, -1):
        end_row = jnp.where(lane < (c + 1) * chunk, ends[c], end_row)
    weight_rows = jnp.exp(end_row - cum)
    dat[0:8, :] = cum
    dat[8:16, :] = weight_rows
    dat[16:24, :] = jnp.exp(cum)
    pos = me * span + lax.broadcasted_iota(jnp.int32, (1, span), 1)
    valid = []
    for u in range(users):
        keep = (pos >= n_ctx * span - hl[u]) & (mk[u : u + 1, :] == 1)
        valid.append(jnp.where(keep, 1.0, 0.0))
    for h in range(heads):
        for u in range(users):
            p = 8 + u * heads + h
            dat[p : p + 1, :] = dat[p : p + 1, :] * valid[u]
    col = jnp.transpose(dat[...])
    tall[me] = jnp.broadcast_to(end_total, (8, 128))

    def right_copy(p):
        return pltpu.make_async_remote_copy(
            src_ref=p_out.at[p],
            dst_ref=p_in.at[p],
            send_sem=p_send.at[p],
            recv_sem=p_recv.at[p],
            device_id={"ctx": lax.rem(me + 1, n_ctx)},
            device_id_type=MESH,
        )

    def left_copy(p):
        return pltpu.make_async_remote_copy(
            src_ref=x_out.at[p],
            dst_ref=x_in.at[p],
            send_sem=x_send.at[p],
            recv_sem=x_recv.at[p],
            device_id={"ctx": lax.rem(me + n_ctx - 1, n_ctx)},
            device_id_type=MESH,
        )

    last = n_ctx - 1

    weight = iw[...]
    gain = ig[...]
    tri = lax.broadcasted_iota(jnp.int32, (chunk, chunk), 0) >= lax.broadcasted_iota(
        jnp.int32, (chunk, chunk), 1
    )

    def place(u, c):
        b = u * chunks + c
        return slice(b * chunk, (b + 1) * chunk), slice(c * chunk, (c + 1) * chunk)

    def keys_values(u):
        ru = slice(u * span, (u + 1) * span)
        rows = normed(be[u], weight, gain)
        norm_s[ru, :] = rows
        key_s[ru, :] = (mm(rows, pw[1]) * DH ** (-0.5)).astype(BF16)
        val_s[ru, :] = mm(rows, pw[2]).astype(BF16)
        for h in range(heads):
            p = u * heads + h
            hc = slice(h * DH, (h + 1) * DH)
            for c in range(chunks):
                r, rc = place(u, c)
                kw = (key_s[r, hc].astype(F32) * col[rc, 8 + p : 9 + p]).astype(BF16)
                lst[p, c] = mm_tn(kw, val_s[r, hc])

    def local_states(u):
        for p in range(u * heads, (u + 1) * heads):
            total = lst[p, 0]
            for c in range(1, chunks):
                total = total * fades[c][p : p + 1, :] + lst[p, c]
            loc[p] = total

    def first_sends(u):
        @pl.when(me == 0)
        def _():
            for p in range(u * heads, (u + 1) * heads):
                p_out[p] = loc[p].astype(p_out.dtype)
                if n_ctx > 1:
                    right_copy(p).start()

        @pl.when(me == last)
        def _():
            for p in range(u * heads, (u + 1) * heads):
                x_out[p] = loc[p].astype(x_out.dtype)
                if n_ctx > 1:
                    left_copy(p).start()

    def relay_right(u):
        for p in range(u * heads, (u + 1) * heads):
            right_copy(p).wait_recv()

            @pl.when(me < last)
            def _():
                p_out[p] = (
                    p_in[p].astype(F32) * fade_total[p : p + 1, :] + loc[p]
                ).astype(p_out.dtype)
                right_copy(p).start()

    def relay_left(u):
        for p in range(u * heads, (u + 1) * heads):
            left_copy(p).wait_recv()

            @pl.when(me > 0)
            def _():
                x_out[p] = (
                    x_in[p].astype(F32) + loc[p] * fade_after[p : p + 1, :]
                ).astype(x_out.dtype)
                left_copy(p).start()

    half = n_ctx // 2

    def near_relay(u):
        if n_ctx > 1:

            @pl.when((me > 0) & (me < half))
            def _():
                relay_right(u)

            @pl.when((me < last) & (me >= half))
            def _():
                relay_left(u)

    def far_relay(u, ends):
        if n_ctx > 1:
            at_end = (me == 0) | (me == last)
            turn = at_end if ends else jnp.logical_not(at_end)

            @pl.when(turn & (me < half))
            def _():
                relay_left(u)

            @pl.when(turn & (me >= half))
            def _():
                relay_right(u)

    def queries_gates(u):
        ru = slice(u * span, (u + 1) * span)
        rows = norm_s[ru, :]
        qry_s[ru, :] = mm(rows, pw[0]).astype(BF16)
        gate_s[ru, :] = silu(mm(rows, pw[3]).astype(BF16).astype(F32)) * out_gain

    def attention(u):
        for c in range(chunks):
            r, rc = place(u, c)
            seen = tri & (valid[u][:, rc] > 0.5)
            for h in range(heads):
                p = u * heads + h
                hc = slice(h * DH, (h + 1) * DH)
                gap = col[rc, p : p + 1] - dat[p : p + 1, rc]
                decay = jnp.where(seen, jnp.exp(jnp.where(tri, gap, 0.0)), 0.0)
                att = (mm_nt(qry_s[r, hc], key_s[r, hc]) * decay).astype(BF16)
                within_s[r, hc] = mm(att, val_s[r, hc])

    @pl.when(me == 0)
    def _():
        p_in[...] = jnp.zeros_like(p_in)

    @pl.when(me == last)
    def _():
        x_in[...] = jnp.zeros_like(x_in)

    t_copies = []
    for k in range(1, n_ctx):
        cp = pltpu.make_async_remote_copy(
            src_ref=tall.at[me],
            dst_ref=tall.at[me],
            send_sem=t_send.at[k],
            recv_sem=t_recv.at[me],
            device_id={"ctx": lax.rem(me + k, n_ctx)},
            device_id_type=MESH,
        )
        cp.start()
        t_copies.append(cp)

    for u in range(users):
        keys_values(u)
        local_states(u)
        first_sends(u)

    for k in range(1, n_ctx):
        src = lax.rem(me + n_ctx - k, n_ctx)
        pltpu.make_async_remote_copy(
            src_ref=tall.at[src],
            dst_ref=tall.at[src],
            send_sem=t_send.at[k],
            recv_sem=t_recv.at[src],
            device_id={"ctx": lax.rem(me + k, n_ctx)},
            device_id_type=MESH,
        ).wait_recv()
    after = jnp.zeros((8, 128), F32)
    for j in range(n_ctx):
        after = after + jnp.where(j > me, tall[j], 0.0)
    fade_after = jnp.exp(after)[:, 0:1]

    for name in ("q", "g", "og", "ce", "r2", "rf"):
        loads[name].wait()
    out_gain = og[...]
    near_relay(0)
    pass_on(range(0, 1))
    for u in range(users):
        queries_gates(u)
    for u in range(1, users):
        near_relay(u)
    pass_on(range(1, 2))
    far_relay(0, False)
    attention(0)
    pass_on(range(2, 3))
    cnorm[...] = normed(ce[...].reshape(users * cand, ce.shape[2]), weight, gain)
    cand_q = mm(cnorm[...], pw[0]).astype(BF16)
    own = cnorm[:, pl.ds(pl.multiple_of(hm * cols, DH), cols)].astype(F32)
    for u in range(1, users):
        far_relay(u, False)
    pass_on(range(3, nx))

    def candidates(u):
        rows = slice(u * cand, (u + 1) * cand)
        for h in range(heads):
            p = u * heads + h
            hc = slice(h * DH, (h + 1) * DH)
            state = p_in[p].astype(F32) * fade_total[p : p + 1, :] + loc[p]
            state = state * fade_after[p : p + 1, :] + x_in[p].astype(F32)
            read = mm(cand_q[rows, hc], state.astype(BF16))
            scale = lax.rsqrt(jnp.mean(read * read, axis=-1, keepdims=True) + EPS)
            feat[u, :, hc] = (read * scale * out_gain[:, hc] + own[rows, hc]).astype(BF16)
        for k in range(1, n_head):
            feat_copy(u, k).start()

    def feat_copy(u, k):
        target = lax.rem(hm + k, n_head)
        return pltpu.make_async_remote_copy(
            src_ref=feat.at[u, pl.ds(pl.multiple_of(target * share, share), share), :],
            dst_ref=feat_in.at[hm, u],
            send_sem=f_send.at[u, k],
            recv_sem=f_recv.at[u, hm],
            device_id={"head": target},
            device_id_type=MESH,
        )

    def histories(u):
        for h in range(heads):
            p = u * heads + h
            hc = slice(h * DH, (h + 1) * DH)
            state = p_in[p].astype(F32)
            for c in range(chunks):
                r, rc = place(u, c)
                read = within_s[r, hc] + col[rc, 16 + p : 17 + p] * mm(
                    qry_s[r, hc], state.astype(BF16)
                )
                scale = lax.rsqrt(jnp.mean(read * read, axis=-1, keepdims=True) + EPS)
                hist[u, rc, hc] = (read * scale * gate_s[r, hc]).astype(BF16)
                if c + 1 < chunks:
                    state = state * fades[c][p : p + 1, :] + lst[p, c]

    for u in range(users):
        far_relay(u, True)
        candidates(u)
        if u + 1 < users:
            attention(u + 1)
            histories(u)

    pass_on_y(range(ny))
    histories(users - 1)

    mine = feat[:, pl.ds(pl.multiple_of(hm * share, share), share), :]
    hidden = mm(mine.reshape(users * share, cols), rank[hm])
    rank_copy(sibling, sibling, 0).wait_recv()
    for k in range(CORES, n_head, CORES):
        src = lax.rem(sibling + n_head - k, n_head)
        for t in range(nx):
            to_sibling(src, k, t, mine_g, t).wait_recv()
        for t in range(ny):
            to_sibling(src, k, t, other_g, nx + t).wait_recv()
    for k in range(1, n_head):
        src = lax.rem(hm + n_head - k, n_head)
        for u in range(users):
            pltpu.make_async_remote_copy(
                src_ref=feat_in.at[src, u],
                dst_ref=feat_in.at[src, u],
                send_sem=f_send.at[u, k],
                recv_sem=f_recv.at[u, src],
                device_id={"head": src},
                device_id_type=MESH,
            ).wait_recv()
        hidden = hidden + mm(feat_in[src].reshape(users * share, cols), rank[src])
    second = r2[...].astype(F32)
    acted = silu(hidden)
    summed = acted[:, 0:128] * second[0:1, :]
    for i in range(1, second.shape[0]):
        summed = summed + acted[:, i * 128 : (i + 1) * 128] * second[i : i + 1, :]
    score_o[...] = jnp.sum(summed.reshape(users, share, 128), axis=-1)

    for cp in t_copies + rank_copies:
        cp.wait_send()
    for u in range(users):
        for k in range(1, n_head):
            feat_copy(u, k).wait_send()
    if n_ctx > 1:

        @pl.when(me < last)
        def _():
            for p in range(pairs):
                right_copy(p).wait_send()

        @pl.when(me > 0)
        def _():
            for p in range(pairs):
                left_copy(p).wait_send()


def results(hist_i, score_i, hist_o, score_o, sem):
    copies = [
        pltpu.make_async_copy(score_i, score_o, sem.at[0]),
    ]
    users = hist_i.shape[0]
    for u in range(users):
        copies.append(pltpu.make_async_copy(hist_i.at[u], hist_o.at[u], sem.at[u + 1]))
    for cp in copies:
        cp.start()
    for cp in copies:
        cp.wait()


def local(
    n_grp,
    n_ctx,
    n_head,
    behavior_embed,
    behavior_mask,
    history_len,
    log_decay,
    candidate_embed,
    input_weight,
    input_gain,
    proj_weight,
    output_gain,
    ranker_first,
    ranker_second,
):
    users, span, embed = behavior_embed.shape
    cand = candidate_embed.shape[1]
    width, cols = proj_weight.shape[1:]
    hidden = ranker_first.shape[1]
    heads = cols // DH
    pairs = heads * users
    chunk = 256 if span % 256 == 0 else 128
    chunks = span // chunk
    share = cand // n_head
    wire = BF16 if n_ctx <= 8 else F32
    rows = users * span
    dma = pltpu.SemaphoreType.DMA
    hbm_spec = pl.BlockSpec(memory_space=pltpu.HBM)
    vmem_spec = pl.BlockSpec(memory_space=pltpu.VMEM)
    flops = 2 * rows * width * (embed + 4 * cols)
    history_out, scores = pl.pallas_call(
        functools.partial(kernel, n_grp, n_ctx, n_head, chunk),
        out_shape=(
            pltpu.VMEM((users, span, cols), BF16),
            pltpu.VMEM((users, share), F32),
        ),
        in_specs=[pl.BlockSpec(memory_space=pltpu.SMEM)] + [hbm_spec] * 10,
        out_specs=(vmem_spec, vmem_spec),
        scratch_shapes=[
            pltpu.VMEM((users, span, embed), BF16),
            pltpu.VMEM((users, span), jnp.int32),
            pltpu.VMEM((heads, users, span), F32),
            pltpu.VMEM((users, cand, embed), BF16),
            pltpu.VMEM((embed, width), BF16),
            pltpu.VMEM((1, width), F32),
            pltpu.VMEM((4, width, cols), BF16),
            pltpu.VMEM((1, cols), F32),
            pltpu.VMEM((hidden // 128, 128), BF16),
            pltpu.VMEM((n_head, cols, hidden), BF16),
            pltpu.VMEM((rows, width), BF16),
            pltpu.VMEM((users * cand, width), BF16),
            pltpu.VMEM((rows, cols), BF16),
            pltpu.VMEM((rows, cols), BF16),
            pltpu.VMEM((rows, cols), BF16),
            pltpu.VMEM((rows, cols), F32),
            pltpu.VMEM((rows, cols), F32),
            pltpu.VMEM((24, span), F32),
            pltpu.VMEM((pairs, chunks, DH, DH), F32),
            pltpu.VMEM((pairs, DH, DH), F32),
            pltpu.VMEM((n_ctx, 8, 128), F32),
            pltpu.VMEM((pairs, DH, DH), wire),
            pltpu.VMEM((pairs, DH, DH), wire),
            pltpu.VMEM((pairs, DH, DH), wire),
            pltpu.VMEM((pairs, DH, DH), wire),
            pltpu.VMEM((users, cand, cols), BF16),
            pltpu.VMEM((n_head, users, share, cols), BF16),
            dma((13,)),
            dma((n_ctx,)),
            dma((n_ctx,)),
            dma((pairs,)),
            dma((pairs,)),
            dma((pairs,)),
            dma((pairs,)),
            dma((2 * n_head,)),
            dma((n_head,)),
            dma((n_head, 8)),
            dma((n_head, 8)),
            dma((n_head, 8)),
            dma((n_head, 8)),
            dma((n_head, 8)),
            dma((n_head, 8)),
            dma((users, n_head)),
            dma((users, n_head)),
        ],
        compiler_params=pltpu.CompilerParams(
            collective_id=0, has_side_effects=True, vmem_limit_bytes=60 * 1024 * 1024
        ),
        cost_estimate=pl.CostEstimate(
            flops=flops, bytes_accessed=6 * 1024 * 1024, transcendentals=0
        ),
    )(
        history_len,
        behavior_embed,
        behavior_mask,
        log_decay,
        candidate_embed,
        input_weight,
        input_gain.reshape(1, width),
        proj_weight,
        output_gain.reshape(1, cols),
        ranker_first,
        ranker_second.reshape(hidden // 128, 128),
    )
    return pl.pallas_call(
        results,
        out_shape=(
            jax.ShapeDtypeStruct(history_out.shape, BF16),
            jax.ShapeDtypeStruct(scores.shape, F32),
        ),
        in_specs=[vmem_spec, vmem_spec],
        out_specs=(hbm_spec, hbm_spec),
        scratch_shapes=[dma((users + 1,))],
        compiler_params=pltpu.CompilerParams(vmem_limit_bytes=8 * 1024 * 1024),
        cost_estimate=pl.CostEstimate(flops=0, bytes_accessed=1024 * 1024, transcendentals=0),
    )(history_out, scores)


def solution(mesh):
    in_specs = (
        P("grp", "ctx", None),
        P("grp", "ctx"),
        P("grp"),
        P("head", "grp", "ctx"),
        P("grp", "ctx", None),
        P(),
        P(),
        P(None, None, "head"),
        P("head"),
        P("head", None),
        P(),
    )
    out_specs = (P("grp", "ctx", "head"), P("grp", ("ctx", "head")))
    return jax.shard_map(
        functools.partial(local, mesh.shape["grp"], mesh.shape["ctx"], mesh.shape["head"]),
        mesh=mesh,
        in_specs=in_specs,
        out_specs=out_specs,
        check_vma=False,
    )
```

```python
import functools

import jax
import jax.numpy as jnp
from jax import lax
from jax.experimental import pallas as pl
from jax.experimental.pallas import tpu as pltpu
from jax.sharding import PartitionSpec as P

DH = 128
CORES = 2
EPS = 1e-05
F32 = jnp.float32
BF16 = jnp.bfloat16
MESH = pl.DeviceIdType.MESH


def mm(a, b):
    return jnp.dot(a, b, preferred_element_type=F32)


def mm_tn(a, b):
    return lax.dot_general(a, b, (((0,), (0,)), ((), ())), preferred_element_type=F32)


def mm_nt(a, b):
    return lax.dot_general(a, b, (((1,), (1,)), ((), ())), preferred_element_type=F32)


def silu(x):
    return x / (1.0 + jnp.exp(-x))


def normed(rows, weight, gain):
    raw = mm(rows, weight).astype(BF16).astype(F32)
    scale = lax.rsqrt(jnp.mean(raw * raw, axis=-1, keepdims=True) + EPS)
    return (raw * scale * gain).astype(BF16)


def kernel(
    n_ctx,
    n_head,
    chunk,
    hl,
    be_h,
    mk_h,
    ld_h,
    ce_h,
    iw_h,
    ig_h,
    pw_h,
    og_h,
    rf_h,
    r2_h,
    hist,
    score_o,
    be,
    mk,
    ld,
    ce,
    iw,
    ig,
    pw,
    og,
    r2,
    rank,
    norm_s,
    cnorm,
    key_s,
    val_s,
    qry_s,
    gate_s,
    within_s,
    dat,
    lst,
    loc,
    tall,
    p_in,
    p_out,
    x_in,
    x_out,
    feat,
    feat_in,
    h_sum,
    h_out,
    h_in,
    load_sem,
    t_send,
    t_recv,
    p_send,
    p_recv,
    x_send,
    x_recv,
    r_send,
    r_recv,
    f_send,
    f_recv,
    h_send,
    h_recv,
):
    users, span, _ = be.shape
    cand = ce.shape[1]
    cols = og.shape[1]
    heads = cols // DH
    pairs = heads * users
    chunks = span // chunk
    share = cand // n_head
    me = lax.axis_index("ctx")
    hm = lax.axis_index("head")
    core = lax.rem(hm, CORES)

    loads = {}
    for i, (name, src, dst) in enumerate(
        (
            ("be", be_h, be),
            ("iw", iw_h, iw),
            ("ig", ig_h, ig),
            ("ld", ld_h, ld),
            ("mk", mk_h, mk),
            ("k", pw_h.at[1], pw.at[1]),
            ("v", pw_h.at[2], pw.at[2]),
            ("q", pw_h.at[0], pw.at[0]),
            ("g", pw_h.at[3], pw.at[3]),
            ("og", og_h, og),
            ("ce", ce_h, ce),
            ("r2", r2_h, r2),
            ("rf", rf_h, rank.at[hm]),
        )
    ):
        loads[name] = pltpu.make_async_copy(src, dst, load_sem.at[i])
        loads[name].start()

    barrier = pltpu.get_barrier_semaphore()
    for k in range(1, n_ctx):
        pl.semaphore_signal(
            barrier, inc=1, device_id={"ctx": lax.rem(me + k, n_ctx)}, device_id_type=MESH
        )
    for k in range(1, n_head):
        pl.semaphore_signal(
            barrier, inc=1, device_id={"head": lax.rem(hm + k, n_head)}, device_id_type=MESH
        )

    pl.semaphore_wait(barrier, n_ctx + n_head - 2)

    def rank_copy(slot, target, sem, src=None):
        return pltpu.make_async_remote_copy(
            src_ref=rank.at[slot] if src is None else src,
            dst_ref=rank.at[slot],
            send_sem=r_send.at[sem],
            recv_sem=r_recv.at[slot],
            device_id={"head": target},
            device_id_type=MESH,
        )

    sibling = hm + 1 - 2 * core
    rank_copies = []
    rank_copies.append(rank_copy(hm, sibling, 0, rf_h))
    rank_copies[-1].start()

    for name in ("ld", "mk", "be", "iw", "ig", "k", "v"):
        loads[name].wait()
    dat[...] = jnp.zeros_like(dat)
    for u in range(users):
        for h in range(heads):
            p = u * heads + h
            dat[p : p + 1, :] = ld[h, u : u + 1, :]
    cum = dat[0:8, :]
    lane = lax.broadcasted_iota(jnp.int32, (8, span), 1)
    in_chunk = lax.rem(lane, chunk)
    step = 1
    while step < chunk:
        cum = cum + jnp.where(in_chunk >= step, pltpu.roll(cum, step, 1), 0.0)
        step *= 2
    ends = [cum[:, (c + 1) * chunk - 1 : (c + 1) * chunk] for c in range(chunks)]
    fades = [jnp.exp(e) for e in ends]
    end_total = functools.reduce(jnp.add, ends)
    fade_total = jnp.exp(end_total)
    end_row = ends[-1]
    for c in range(chunks - 2, -1, -1):
        end_row = jnp.where(lane < (c + 1) * chunk, ends[c], end_row)
    weight_rows = jnp.exp(end_row - cum)
    dat[0:8, :] = cum
    dat[8:16, :] = weight_rows
    dat[16:24, :] = jnp.exp(cum)
    pos = me * span + lax.broadcasted_iota(jnp.int32, (1, span), 1)
    valid = []
    for u in range(users):
        keep = (pos >= n_ctx * span - hl[u]) & (mk[u : u + 1, :] == 1)
        valid.append(jnp.where(keep, 1.0, 0.0))
    for h in range(heads):
        for u in range(users):
            p = 8 + u * heads + h
            dat[p : p + 1, :] = dat[p : p + 1, :] * valid[u]
    col = jnp.transpose(dat[...])
    tall[me] = jnp.broadcast_to(end_total, (8, 128))

    def right_copy(p):
        return pltpu.make_async_remote_copy(
            src_ref=p_out.at[p],
            dst_ref=p_in.at[p],
            send_sem=p_send.at[p],
            recv_sem=p_recv.at[p],
            device_id={"ctx": lax.rem(me + 1, n_ctx)},
            device_id_type=MESH,
        )

    def left_copy(p):
        return pltpu.make_async_remote_copy(
            src_ref=x_out.at[p],
            dst_ref=x_in.at[p],
            send_sem=x_send.at[p],
            recv_sem=x_recv.at[p],
            device_id={"ctx": lax.rem(me + n_ctx - 1, n_ctx)},
            device_id_type=MESH,
        )

    last = n_ctx - 1

    weight = iw[...]
    gain = ig[...]
    tri = lax.broadcasted_iota(jnp.int32, (chunk, chunk), 0) >= lax.broadcasted_iota(
        jnp.int32, (chunk, chunk), 1
    )

    def place(u, c):
        b = u * chunks + c
        return slice(b * chunk, (b + 1) * chunk), slice(c * chunk, (c + 1) * chunk)

    def keys_values(u):
        ru = slice(u * span, (u + 1) * span)
        rows = normed(be[u], weight, gain)
        norm_s[ru, :] = rows
        key_s[ru, :] = (mm(rows, pw[1]) * DH ** (-0.5)).astype(BF16)
        val_s[ru, :] = mm(rows, pw[2]).astype(BF16)
        for h in range(heads):
            p = u * heads + h
            hc = slice(h * DH, (h + 1) * DH)
            for c in range(chunks):
                r, rc = place(u, c)
                kw = (key_s[r, hc].astype(F32) * col[rc, 8 + p : 9 + p]).astype(BF16)
                lst[p, c] = mm_tn(kw, val_s[r, hc])

    def local_states(u):
        for p in range(u * heads, (u + 1) * heads):
            total = lst[p, 0]
            for c in range(1, chunks):
                total = total * fades[c][p : p + 1, :] + lst[p, c]
            loc[p] = total

    def first_sends(u):
        @pl.when(me == 0)
        def _():
            for p in range(u * heads, (u + 1) * heads):
                p_out[p] = loc[p].astype(p_out.dtype)
                if n_ctx > 1:
                    right_copy(p).start()

        @pl.when(me == last)
        def _():
            for p in range(u * heads, (u + 1) * heads):
                x_out[p] = loc[p].astype(x_out.dtype)
                if n_ctx > 1:
                    left_copy(p).start()

    def relay_right(u):
        for p in range(u * heads, (u + 1) * heads):
            right_copy(p).wait_recv()

            @pl.when(me < last)
            def _():
                p_out[p] = (
                    p_in[p].astype(F32) * fade_total[p : p + 1, :] + loc[p]
                ).astype(p_out.dtype)
                right_copy(p).start()

    def relay_left(u):
        for p in range(u * heads, (u + 1) * heads):
            left_copy(p).wait_recv()

            @pl.when(me > 0)
            def _():
                x_out[p] = (
                    x_in[p].astype(F32) + loc[p] * fade_after[p : p + 1, :]
                ).astype(x_out.dtype)
                left_copy(p).start()

    half = n_ctx // 2

    def near_relay(u):
        if n_ctx > 1:

            @pl.when((me > 0) & (me < half))
            def _():
                relay_right(u)

            @pl.when((me < last) & (me >= half))
            def _():
                relay_left(u)

    def far_relay(u, ends):
        if n_ctx > 1:
            at_end = (me == 0) | (me == last)
            turn = at_end if ends else jnp.logical_not(at_end)

            @pl.when(turn & (me < half))
            def _():
                relay_left(u)

            @pl.when(turn & (me >= half))
            def _():
                relay_right(u)

    def queries_gates(u):
        ru = slice(u * span, (u + 1) * span)
        rows = norm_s[ru, :]
        qry_s[ru, :] = mm(rows, pw[0]).astype(BF16)
        gate_s[ru, :] = silu(mm(rows, pw[3]).astype(BF16).astype(F32)) * out_gain

    def attention(u):
        for c in range(chunks):
            r, rc = place(u, c)
            seen = tri & (valid[u][:, rc] > 0.5)
            for h in range(heads):
                p = u * heads + h
                hc = slice(h * DH, (h + 1) * DH)
                gap = col[rc, p : p + 1] - dat[p : p + 1, rc]
                decay = jnp.where(seen, jnp.exp(jnp.where(tri, gap, 0.0)), 0.0)
                att = (mm_nt(qry_s[r, hc], key_s[r, hc]) * decay).astype(BF16)
                within_s[r, hc] = mm(att, val_s[r, hc])

    @pl.when(me == 0)
    def _():
        p_in[...] = jnp.zeros_like(p_in)

    @pl.when(me == last)
    def _():
        x_in[...] = jnp.zeros_like(x_in)

    t_copies = []
    for k in range(1, n_ctx):
        cp = pltpu.make_async_remote_copy(
            src_ref=tall.at[me],
            dst_ref=tall.at[me],
            send_sem=t_send.at[k],
            recv_sem=t_recv.at[me],
            device_id={"ctx": lax.rem(me + k, n_ctx)},
            device_id_type=MESH,
        )
        cp.start()
        t_copies.append(cp)

    for u in range(users):
        keys_values(u)
        local_states(u)
        first_sends(u)

    for k in range(1, n_ctx):
        src = lax.rem(me + n_ctx - k, n_ctx)
        pltpu.make_async_remote_copy(
            src_ref=tall.at[src],
            dst_ref=tall.at[src],
            send_sem=t_send.at[k],
            recv_sem=t_recv.at[src],
            device_id={"ctx": lax.rem(me + k, n_ctx)},
            device_id_type=MESH,
        ).wait_recv()
    after = jnp.zeros((8, 128), F32)
    for j in range(n_ctx):
        after = after + jnp.where(j > me, tall[j], 0.0)
    fade_after = jnp.exp(after)[:, 0:1]

    for name in ("q", "g", "og", "ce", "r2", "rf"):
        loads[name].wait()
    out_gain = og[...]
    near_relay(0)
    for u in range(users):
        queries_gates(u)
    for u in range(1, users):
        near_relay(u)
    far_relay(0, False)
    attention(0)
    cnorm[...] = normed(ce[...].reshape(users * cand, ce.shape[2]), weight, gain)
    cand_q = mm(cnorm[...], pw[0]).astype(BF16)
    own = cnorm[:, pl.ds(pl.multiple_of(hm * cols, DH), cols)].astype(F32)
    for u in range(1, users):
        far_relay(u, False)

    chips = n_head // CORES
    chip = hm // CORES
    rank_copy(sibling, sibling, 0).wait_recv()

    def candidates(u):
        rows = slice(u * cand, (u + 1) * cand)
        for h in range(heads):
            p = u * heads + h
            hc = slice(h * DH, (h + 1) * DH)
            state = p_in[p].astype(F32) * fade_total[p : p + 1, :] + loc[p]
            state = state * fade_after[p : p + 1, :] + x_in[p].astype(F32)
            read = mm(cand_q[rows, hc], state.astype(BF16))
            scale = lax.rsqrt(jnp.mean(read * read, axis=-1, keepdims=True) + EPS)
            feat[u, :, hc] = (read * scale * out_gain[:, hc] + own[rows, hc]).astype(BF16)
        for x in range(chips):
            feat_copy(u, x).start()

    def feat_copy(u, x):
        row = (CORES * x + 1 - core) * share
        return pltpu.make_async_remote_copy(
            src_ref=feat.at[u, pl.ds(pl.multiple_of(row, share), share), :],
            dst_ref=feat_in.at[u, x],
            send_sem=f_send.at[u, x],
            recv_sem=f_recv.at[u, x],
            device_id={"head": sibling},
            device_id_type=MESH,
        )

    def chip_sums(u):
        rows = []
        for x in range(chips):
            row = (CORES * x + core) * share
            rows.append(feat[u, pl.ds(pl.multiple_of(row, share), share), :])
        part = mm(jnp.concatenate(rows, axis=0), rank[hm])
        for x in range(chips):
            feat_copy(u, x).wait_recv()
        part = part + mm(feat_in[u].reshape(chips * share, cols), rank[sibling])
        part = part.reshape(chips, share, part.shape[1])
        h_sum[u] = part
        h_out[u] = part.astype(BF16)
        for k in range(1, chips):
            sum_copy(u, k).start()

    def sum_copy(u, k):
        to = lax.rem(chip + k, chips)
        return pltpu.make_async_remote_copy(
            src_ref=h_out.at[u, to],
            dst_ref=h_in.at[u, chip],
            send_sem=h_send.at[u, k],
            recv_sem=h_recv.at[u, chip],
            device_id={"head": CORES * to + core},
            device_id_type=MESH,
        )

    def histories(u):
        for h in range(heads):
            p = u * heads + h
            hc = slice(h * DH, (h + 1) * DH)
            state = p_in[p].astype(F32)
            for c in range(chunks):
                r, rc = place(u, c)
                read = within_s[r, hc] + col[rc, 16 + p : 17 + p] * mm(
                    qry_s[r, hc], state.astype(BF16)
                )
                scale = lax.rsqrt(jnp.mean(read * read, axis=-1, keepdims=True) + EPS)
                hist[u, rc, hc] = (read * scale * gate_s[r, hc]).astype(BF16)
                if c + 1 < chunks:
                    state = state * fades[c][p : p + 1, :] + lst[p, c]

    for u in range(users):
        far_relay(u, True)
        candidates(u)
        if u + 1 < users:
            attention(u + 1)
        else:
            for v in range(users - 1):
                histories(v)
        chip_sums(u)
    histories(users - 1)

    totals = []
    for u in range(users):
        total = h_sum[u, chip]
        for k in range(1, chips):
            src = lax.rem(chip + chips - k, chips)
            pltpu.make_async_remote_copy(
                src_ref=h_in.at[u, src],
                dst_ref=h_in.at[u, src],
                send_sem=h_send.at[u, k],
                recv_sem=h_recv.at[u, src],
                device_id={"head": CORES * src + core},
                device_id_type=MESH,
            ).wait_recv()
            total = total + h_in[u, src].astype(F32)
        totals.append(total)
    hidden = jnp.concatenate(totals, axis=0)
    second = r2[...].astype(F32)
    acted = silu(hidden)
    summed = acted[:, 0:128] * second[0:1, :]
    for i in range(1, second.shape[0]):
        summed = summed + acted[:, i * 128 : (i + 1) * 128] * second[i : i + 1, :]
    score_o[...] = jnp.sum(summed.reshape(users, share, 128), axis=-1)

    for cp in t_copies + rank_copies:
        cp.wait_send()
    for u in range(users):
        for x in range(chips):
            feat_copy(u, x).wait_send()
        for k in range(1, chips):
            sum_copy(u, k).wait_send()
    if n_ctx > 1:

        @pl.when(me < last)
        def _():
            for p in range(pairs):
                right_copy(p).wait_send()

        @pl.when(me > 0)
        def _():
            for p in range(pairs):
                left_copy(p).wait_send()


def results(hist_i, score_i, hist_o, score_o, sem):
    copies = [
        pltpu.make_async_copy(score_i, score_o, sem.at[0]),
    ]
    users = hist_i.shape[0]
    for u in range(users):
        copies.append(pltpu.make_async_copy(hist_i.at[u], hist_o.at[u], sem.at[u + 1]))
    for cp in copies:
        cp.start()
    for cp in copies:
        cp.wait()


def local(
    n_ctx,
    n_head,
    behavior_embed,
    behavior_mask,
    history_len,
    log_decay,
    candidate_embed,
    input_weight,
    input_gain,
    proj_weight,
    output_gain,
    ranker_first,
    ranker_second,
):
    users, span, embed = behavior_embed.shape
    cand = candidate_embed.shape[1]
    width, cols = proj_weight.shape[1:]
    hidden = ranker_first.shape[1]
    heads = cols // DH
    pairs = heads * users
    chunk = 256 if span % 256 == 0 else 128
    chunks = span // chunk
    share = cand // n_head
    wire = BF16 if n_ctx <= 8 else F32
    rows = users * span
    dma = pltpu.SemaphoreType.DMA
    hbm_spec = pl.BlockSpec(memory_space=pltpu.HBM)
    vmem_spec = pl.BlockSpec(memory_space=pltpu.VMEM)
    flops = 2 * rows * width * (embed + 4 * cols)
    history_out, scores = pl.pallas_call(
        functools.partial(kernel, n_ctx, n_head, chunk),
        out_shape=(
            pltpu.VMEM((users, span, cols), BF16),
            pltpu.VMEM((users, share), F32),
        ),
        in_specs=[pl.BlockSpec(memory_space=pltpu.SMEM)] + [hbm_spec] * 10,
        out_specs=(vmem_spec, vmem_spec),
        scratch_shapes=[
            pltpu.VMEM((users, span, embed), BF16),
            pltpu.VMEM((users, span), jnp.int32),
            pltpu.VMEM((heads, users, span), F32),
            pltpu.VMEM((users, cand, embed), BF16),
            pltpu.VMEM((embed, width), BF16),
            pltpu.VMEM((1, width), F32),
            pltpu.VMEM((4, width, cols), BF16),
            pltpu.VMEM((1, cols), F32),
            pltpu.VMEM((hidden // 128, 128), BF16),
            pltpu.VMEM((n_head, cols, hidden), BF16),
            pltpu.VMEM((rows, width), BF16),
            pltpu.VMEM((users * cand, width), BF16),
            pltpu.VMEM((rows, cols), BF16),
            pltpu.VMEM((rows, cols), BF16),
            pltpu.VMEM((rows, cols), BF16),
            pltpu.VMEM((rows, cols), F32),
            pltpu.VMEM((rows, cols), F32),
            pltpu.VMEM((24, span), F32),
            pltpu.VMEM((pairs, chunks, DH, DH), F32),
            pltpu.VMEM((pairs, DH, DH), F32),
            pltpu.VMEM((n_ctx, 8, 128), F32),
            pltpu.VMEM((pairs, DH, DH), wire),
            pltpu.VMEM((pairs, DH, DH), wire),
            pltpu.VMEM((pairs, DH, DH), wire),
            pltpu.VMEM((pairs, DH, DH), wire),
            pltpu.VMEM((users, cand, cols), BF16),
            pltpu.VMEM((users, n_head // CORES, share, cols), BF16),
            pltpu.VMEM((users, n_head // CORES, share, hidden), F32),
            pltpu.VMEM((users, n_head // CORES, share, hidden), BF16),
            pltpu.VMEM((users, n_head // CORES, share, hidden), BF16),
            dma((13,)),
            dma((n_ctx,)),
            dma((n_ctx,)),
            dma((pairs,)),
            dma((pairs,)),
            dma((pairs,)),
            dma((pairs,)),
            dma((2 * n_head,)),
            dma((n_head,)),
            dma((users, n_head)),
            dma((users, n_head)),
            dma((users, n_head)),
            dma((users, n_head)),
        ],
        compiler_params=pltpu.CompilerParams(
            collective_id=0, has_side_effects=True, vmem_limit_bytes=60 * 1024 * 1024
        ),
        cost_estimate=pl.CostEstimate(
            flops=flops, bytes_accessed=6 * 1024 * 1024, transcendentals=0
        ),
    )(
        history_len,
        behavior_embed,
        behavior_mask,
        log_decay,
        candidate_embed,
        input_weight,
        input_gain.reshape(1, width),
        proj_weight,
        output_gain.reshape(1, cols),
        ranker_first,
        ranker_second.reshape(hidden // 128, 128),
    )
    return pl.pallas_call(
        results,
        out_shape=(
            jax.ShapeDtypeStruct(history_out.shape, BF16),
            jax.ShapeDtypeStruct(scores.shape, F32),
        ),
        in_specs=[vmem_spec, vmem_spec],
        out_specs=(hbm_spec, hbm_spec),
        scratch_shapes=[dma((users + 1,))],
        compiler_params=pltpu.CompilerParams(vmem_limit_bytes=8 * 1024 * 1024),
        cost_estimate=pl.CostEstimate(flops=0, bytes_accessed=1024 * 1024, transcendentals=0),
    )(history_out, scores)


def solution(mesh):
    in_specs = (
        P("grp", "ctx", None),
        P("grp", "ctx"),
        P("grp"),
        P("head", "grp", "ctx"),
        P("grp", "ctx", None),
        P(),
        P(),
        P(None, None, "head"),
        P("head"),
        P("head", None),
        P(),
    )
    out_specs = (P("grp", "ctx", "head"), P("grp", ("ctx", "head")))
    return jax.shard_map(
        functools.partial(local, mesh.shape["ctx"], mesh.shape["head"]),
        mesh=mesh,
        in_specs=in_specs,
        out_specs=out_specs,
        check_vma=False,
    )
```

```python
import functools

import jax
import jax.numpy as jnp
from jax import lax
from jax.experimental import pallas as pl
from jax.experimental.pallas import tpu as pltpu
from jax.sharding import PartitionSpec as P

DH = 128
CORES = 2
EPS = 1e-05
F32 = jnp.float32
BF16 = jnp.bfloat16
MESH = pl.DeviceIdType.MESH


def mm(a, b):
    return jnp.dot(a, b, preferred_element_type=F32)


def mm_tn(a, b):
    return lax.dot_general(a, b, (((0,), (0,)), ((), ())), preferred_element_type=F32)


def mm_nt(a, b):
    return lax.dot_general(a, b, (((1,), (1,)), ((), ())), preferred_element_type=F32)


def silu(x):
    return x / (1.0 + jnp.exp(-x))


def normed(rows, weight, gain):
    raw = mm(rows, weight).astype(BF16).astype(F32)
    scale = lax.rsqrt(jnp.mean(raw * raw, axis=-1, keepdims=True) + EPS)
    return (raw * scale * gain).astype(BF16)


def kernel(
    n_ctx,
    n_head,
    chunk,
    hl,
    be_h,
    mk_h,
    ld_h,
    ce_h,
    iw_h,
    ig_h,
    pw_h,
    og_h,
    rf_h,
    r2_h,
    hist,
    score_o,
    be,
    mk,
    ld,
    ce,
    iw,
    ig,
    pw,
    og,
    r2,
    rank,
    norm_s,
    cnorm,
    key_s,
    val_s,
    qry_s,
    gate_s,
    within_s,
    dat,
    lst,
    loc,
    tall,
    p_in,
    p_out,
    x_in,
    x_out,
    feat,
    feat_in,
    load_sem,
    t_send,
    t_recv,
    p_send,
    p_recv,
    x_send,
    x_recv,
    r_send,
    r_recv,
    f_send,
    f_recv,
):
    users, span, _ = be.shape
    cand = ce.shape[1]
    cols = og.shape[1]
    heads = cols // DH
    pairs = heads * users
    chunks = span // chunk
    share = cand // n_head
    me = lax.axis_index("ctx")
    hm = lax.axis_index("head")
    core = lax.rem(hm, CORES)

    loads = {}
    for i, (name, src, dst) in enumerate(
        (
            ("be", be_h, be),
            ("iw", iw_h, iw),
            ("ig", ig_h, ig),
            ("ld", ld_h, ld),
            ("mk", mk_h, mk),
            ("k", pw_h.at[1], pw.at[1]),
            ("v", pw_h.at[2], pw.at[2]),
            ("q", pw_h.at[0], pw.at[0]),
            ("g", pw_h.at[3], pw.at[3]),
            ("og", og_h, og),
            ("ce", ce_h, ce),
            ("r2", r2_h, r2),
            ("rf", rf_h, rank.at[hm]),
        )
    ):
        loads[name] = pltpu.make_async_copy(src, dst, load_sem.at[i])
        loads[name].start()

    barrier = pltpu.get_barrier_semaphore()
    for k in range(1, n_ctx):
        pl.semaphore_signal(
            barrier, inc=1, device_id={"ctx": lax.rem(me + k, n_ctx)}, device_id_type=MESH
        )
    for k in range(1, n_head):
        pl.semaphore_signal(
            barrier, inc=1, device_id={"head": lax.rem(hm + k, n_head)}, device_id_type=MESH
        )

    pl.semaphore_wait(barrier, n_ctx + n_head - 2)

    def rank_copy(slot, target, sem, src=None):
        return pltpu.make_async_remote_copy(
            src_ref=rank.at[slot] if src is None else src,
            dst_ref=rank.at[slot],
            send_sem=r_send.at[sem],
            recv_sem=r_recv.at[slot],
            device_id={"head": target},
            device_id_type=MESH,
        )

    sibling = hm + 1 - 2 * core
    rank_copies = []
    for k in range(CORES, n_head, CORES):
        rank_copies.append(rank_copy(hm, lax.rem(hm + k, n_head), k, rf_h))
        rank_copies[-1].start()
    rank_copies.append(rank_copy(hm, sibling, 0, rf_h))
    rank_copies[-1].start()

    for name in ("ld", "mk", "be", "iw", "ig", "k", "v"):
        loads[name].wait()
    dat[...] = jnp.zeros_like(dat)
    for u in range(users):
        for h in range(heads):
            p = u * heads + h
            dat[p : p + 1, :] = ld[h, u : u + 1, :]
    cum = dat[0:8, :]
    lane = lax.broadcasted_iota(jnp.int32, (8, span), 1)
    in_chunk = lax.rem(lane, chunk)
    step = 1
    while step < chunk:
        cum = cum + jnp.where(in_chunk >= step, pltpu.roll(cum, step, 1), 0.0)
        step *= 2
    ends = [cum[:, (c + 1) * chunk - 1 : (c + 1) * chunk] for c in range(chunks)]
    fades = [jnp.exp(e) for e in ends]
    end_total = functools.reduce(jnp.add, ends)
    fade_total = jnp.exp(end_total)
    end_row = ends[-1]
    for c in range(chunks - 2, -1, -1):
        end_row = jnp.where(lane < (c + 1) * chunk, ends[c], end_row)
    weight_rows = jnp.exp(end_row - cum)
    dat[0:8, :] = cum
    dat[8:16, :] = weight_rows
    dat[16:24, :] = jnp.exp(cum)
    pos = me * span + lax.broadcasted_iota(jnp.int32, (1, span), 1)
    valid = []
    for u in range(users):
        keep = (pos >= n_ctx * span - hl[u]) & (mk[u : u + 1, :] == 1)
        valid.append(jnp.where(keep, 1.0, 0.0))
    for h in range(heads):
        for u in range(users):
            p = 8 + u * heads + h
            dat[p : p + 1, :] = dat[p : p + 1, :] * valid[u]
    col = jnp.transpose(dat[...])
    tall[me] = jnp.broadcast_to(end_total, (8, 128))

    def right_copy(p):
        return pltpu.make_async_remote_copy(
            src_ref=p_out.at[p],
            dst_ref=p_in.at[p],
            send_sem=p_send.at[p],
            recv_sem=p_recv.at[p],
            device_id={"ctx": lax.rem(me + 1, n_ctx)},
            device_id_type=MESH,
        )

    def left_copy(p):
        return pltpu.make_async_remote_copy(
            src_ref=x_out.at[p],
            dst_ref=x_in.at[p],
            send_sem=x_send.at[p],
            recv_sem=x_recv.at[p],
            device_id={"ctx": lax.rem(me + n_ctx - 1, n_ctx)},
            device_id_type=MESH,
        )

    last = n_ctx - 1

    weight = iw[...]
    gain = ig[...]
    tri = lax.broadcasted_iota(jnp.int32, (chunk, chunk), 0) >= lax.broadcasted_iota(
        jnp.int32, (chunk, chunk), 1
    )

    def place(u, c):
        b = u * chunks + c
        return slice(b * chunk, (b + 1) * chunk), slice(c * chunk, (c + 1) * chunk)

    def keys_values(u):
        ru = slice(u * span, (u + 1) * span)
        rows = normed(be[u], weight, gain)
        norm_s[ru, :] = rows
        key_s[ru, :] = (mm(rows, pw[1]) * DH ** (-0.5)).astype(BF16)
        val_s[ru, :] = mm(rows, pw[2]).astype(BF16)
        for h in range(heads):
            p = u * heads + h
            hc = slice(h * DH, (h + 1) * DH)
            for c in range(chunks):
                r, rc = place(u, c)
                kw = (key_s[r, hc].astype(F32) * col[rc, 8 + p : 9 + p]).astype(BF16)
                lst[p, c] = mm_tn(kw, val_s[r, hc])

    def local_states(u):
        for p in range(u * heads, (u + 1) * heads):
            total = lst[p, 0]
            for c in range(1, chunks):
                total = total * fades[c][p : p + 1, :] + lst[p, c]
            loc[p] = total

    def first_sends(u):
        @pl.when(me == 0)
        def _():
            for p in range(u * heads, (u + 1) * heads):
                p_out[p] = loc[p].astype(p_out.dtype)
                if n_ctx > 1:
                    right_copy(p).start()

        @pl.when(me == last)
        def _():
            for p in range(u * heads, (u + 1) * heads):
                x_out[p] = loc[p].astype(x_out.dtype)
                if n_ctx > 1:
                    left_copy(p).start()

    def relay_right(u):
        for p in range(u * heads, (u + 1) * heads):
            right_copy(p).wait_recv()

            @pl.when(me < last)
            def _():
                p_out[p] = (
                    p_in[p].astype(F32) * fade_total[p : p + 1, :] + loc[p]
                ).astype(p_out.dtype)
                right_copy(p).start()

    def relay_left(u):
        for p in range(u * heads, (u + 1) * heads):
            left_copy(p).wait_recv()

            @pl.when(me > 0)
            def _():
                x_out[p] = (
                    x_in[p].astype(F32) + loc[p] * fade_after[p : p + 1, :]
                ).astype(x_out.dtype)
                left_copy(p).start()

    half = n_ctx // 2

    def near_relay(u):
        if n_ctx > 1:

            @pl.when((me > 0) & (me < half))
            def _():
                relay_right(u)

            @pl.when((me < last) & (me >= half))
            def _():
                relay_left(u)

    def far_relay(u, ends):
        if n_ctx > 1:
            at_end = (me == 0) | (me == last)
            turn = at_end if ends else jnp.logical_not(at_end)

            @pl.when(turn & (me < half))
            def _():
                relay_left(u)

            @pl.when(turn & (me >= half))
            def _():
                relay_right(u)

    def queries_gates(u):
        ru = slice(u * span, (u + 1) * span)
        rows = norm_s[ru, :]
        qry_s[ru, :] = mm(rows, pw[0]).astype(BF16)
        gate_s[ru, :] = silu(mm(rows, pw[3]).astype(BF16).astype(F32)) * out_gain

    def attention(u):
        for c in range(chunks):
            r, rc = place(u, c)
            seen = tri & (valid[u][:, rc] > 0.5)
            for h in range(heads):
                p = u * heads + h
                hc = slice(h * DH, (h + 1) * DH)
                gap = col[rc, p : p + 1] - dat[p : p + 1, rc]
                decay = jnp.where(seen, jnp.exp(jnp.where(tri, gap, 0.0)), 0.0)
                att = (mm_nt(qry_s[r, hc], key_s[r, hc]) * decay).astype(BF16)
                within_s[r, hc] = mm(att, val_s[r, hc])

    @pl.when(me == 0)
    def _():
        p_in[...] = jnp.zeros_like(p_in)

    @pl.when(me == last)
    def _():
        x_in[...] = jnp.zeros_like(x_in)

    t_copies = []
    for k in range(1, n_ctx):
        cp = pltpu.make_async_remote_copy(
            src_ref=tall.at[me],
            dst_ref=tall.at[me],
            send_sem=t_send.at[k],
            recv_sem=t_recv.at[me],
            device_id={"ctx": lax.rem(me + k, n_ctx)},
            device_id_type=MESH,
        )
        cp.start()
        t_copies.append(cp)

    for u in range(users):
        keys_values(u)
        local_states(u)
        first_sends(u)

    for k in range(1, n_ctx):
        src = lax.rem(me + n_ctx - k, n_ctx)
        pltpu.make_async_remote_copy(
            src_ref=tall.at[src],
            dst_ref=tall.at[src],
            send_sem=t_send.at[k],
            recv_sem=t_recv.at[src],
            device_id={"ctx": lax.rem(me + k, n_ctx)},
            device_id_type=MESH,
        ).wait_recv()
    after = jnp.zeros((8, 128), F32)
    for j in range(n_ctx):
        after = after + jnp.where(j > me, tall[j], 0.0)
    fade_after = jnp.exp(after)[:, 0:1]

    for name in ("q", "g", "og", "ce", "r2", "rf"):
        loads[name].wait()
    out_gain = og[...]
    near_relay(0)
    for u in range(users):
        queries_gates(u)
    for u in range(1, users):
        near_relay(u)
    far_relay(0, False)
    attention(0)
    cnorm[...] = normed(ce[...].reshape(users * cand, ce.shape[2]), weight, gain)
    cand_q = mm(cnorm[...], pw[0]).astype(BF16)
    own = cnorm[:, pl.ds(pl.multiple_of(hm * cols, DH), cols)].astype(F32)
    for u in range(1, users):
        far_relay(u, False)

    def candidates(u):
        rows = slice(u * cand, (u + 1) * cand)
        for h in range(heads):
            p = u * heads + h
            hc = slice(h * DH, (h + 1) * DH)
            state = p_in[p].astype(F32) * fade_total[p : p + 1, :] + loc[p]
            state = state * fade_after[p : p + 1, :] + x_in[p].astype(F32)
            read = mm(cand_q[rows, hc], state.astype(BF16))
            scale = lax.rsqrt(jnp.mean(read * read, axis=-1, keepdims=True) + EPS)
            feat[u, :, hc] = (read * scale * out_gain[:, hc] + own[rows, hc]).astype(BF16)
        for k in range(1, n_head):
            feat_copy(u, k).start()

    def feat_copy(u, k):
        target = lax.rem(hm + k, n_head)
        return pltpu.make_async_remote_copy(
            src_ref=feat.at[u, pl.ds(pl.multiple_of(target * share, share), share), :],
            dst_ref=feat_in.at[hm, u],
            send_sem=f_send.at[u, k],
            recv_sem=f_recv.at[u, hm],
            device_id={"head": target},
            device_id_type=MESH,
        )

    def histories(u):
        for h in range(heads):
            p = u * heads + h
            hc = slice(h * DH, (h + 1) * DH)
            state = p_in[p].astype(F32)
            for c in range(chunks):
                r, rc = place(u, c)
                read = within_s[r, hc] + col[rc, 16 + p : 17 + p] * mm(
                    qry_s[r, hc], state.astype(BF16)
                )
                scale = lax.rsqrt(jnp.mean(read * read, axis=-1, keepdims=True) + EPS)
                hist[u, rc, hc] = (read * scale * gate_s[r, hc]).astype(BF16)
                if c + 1 < chunks:
                    state = state * fades[c][p : p + 1, :] + lst[p, c]

    def pass_on():
        for k in range(CORES, n_head, CORES):
            src = lax.rem(hm + n_head - k, n_head)
            rank_copy(src, sibling, k).wait_recv()
            rank_copies.append(rank_copy(src, sibling, n_head + k))
            rank_copies[-1].start()

    for u in range(users):
        if u == users - 1:
            pass_on()
        far_relay(u, True)
        candidates(u)
        if u + 1 < users:
            attention(u + 1)
            histories(u)

    histories(users - 1)

    mine = feat[:, pl.ds(pl.multiple_of(hm * share, share), share), :]
    hidden = mm(mine.reshape(users * share, cols), rank[hm])
    rank_copy(sibling, sibling, 0).wait_recv()
    direct = [lax.rem(hm + n_head - k, n_head) for k in range(CORES, n_head, CORES)]
    passed = [lax.rem(sibling + n_head - k, n_head) for k in range(CORES, n_head, CORES)]
    for i, src in enumerate([sibling] + direct + passed):
        if i > len(direct):
            k = CORES * (i - len(direct))
            rank_copy(src, sibling, n_head + k).wait_recv()
        for u in range(users):
            pltpu.make_async_remote_copy(
                src_ref=feat_in.at[src, u],
                dst_ref=feat_in.at[src, u],
                send_sem=f_send.at[u, 0],
                recv_sem=f_recv.at[u, src],
                device_id={"head": src},
                device_id_type=MESH,
            ).wait_recv()
        hidden = hidden + mm(feat_in[src].reshape(users * share, cols), rank[src])
    second = r2[...].astype(F32)
    acted = silu(hidden)
    summed = acted[:, 0:128] * second[0:1, :]
    for i in range(1, second.shape[0]):
        summed = summed + acted[:, i * 128 : (i + 1) * 128] * second[i : i + 1, :]
    score_o[...] = jnp.sum(summed.reshape(users, share, 128), axis=-1)

    for cp in t_copies + rank_copies:
        cp.wait_send()
    for u in range(users):
        for k in range(1, n_head):
            feat_copy(u, k).wait_send()
    if n_ctx > 1:

        @pl.when(me < last)
        def _():
            for p in range(pairs):
                right_copy(p).wait_send()

        @pl.when(me > 0)
        def _():
            for p in range(pairs):
                left_copy(p).wait_send()


def results(hist_i, score_i, hist_o, score_o, sem):
    copies = [
        pltpu.make_async_copy(score_i, score_o, sem.at[0]),
    ]
    users = hist_i.shape[0]
    for u in range(users):
        copies.append(pltpu.make_async_copy(hist_i.at[u], hist_o.at[u], sem.at[u + 1]))
    for cp in copies:
        cp.start()
    for cp in copies:
        cp.wait()


def local(
    n_ctx,
    n_head,
    behavior_embed,
    behavior_mask,
    history_len,
    log_decay,
    candidate_embed,
    input_weight,
    input_gain,
    proj_weight,
    output_gain,
    ranker_first,
    ranker_second,
):
    users, span, embed = behavior_embed.shape
    cand = candidate_embed.shape[1]
    width, cols = proj_weight.shape[1:]
    hidden = ranker_first.shape[1]
    heads = cols // DH
    pairs = heads * users
    chunk = 256 if span % 256 == 0 else 128
    chunks = span // chunk
    share = cand // n_head
    wire = BF16 if n_ctx <= 8 else F32
    rows = users * span
    dma = pltpu.SemaphoreType.DMA
    hbm_spec = pl.BlockSpec(memory_space=pltpu.HBM)
    vmem_spec = pl.BlockSpec(memory_space=pltpu.VMEM)
    flops = 2 * rows * width * (embed + 4 * cols)
    history_out, scores = pl.pallas_call(
        functools.partial(kernel, n_ctx, n_head, chunk),
        out_shape=(
            pltpu.VMEM((users, span, cols), BF16),
            pltpu.VMEM((users, share), F32),
        ),
        in_specs=[pl.BlockSpec(memory_space=pltpu.SMEM)] + [hbm_spec] * 10,
        out_specs=(vmem_spec, vmem_spec),
        scratch_shapes=[
            pltpu.VMEM((users, span, embed), BF16),
            pltpu.VMEM((users, span), jnp.int32),
            pltpu.VMEM((heads, users, span), F32),
            pltpu.VMEM((users, cand, embed), BF16),
            pltpu.VMEM((embed, width), BF16),
            pltpu.VMEM((1, width), F32),
            pltpu.VMEM((4, width, cols), BF16),
            pltpu.VMEM((1, cols), F32),
            pltpu.VMEM((hidden // 128, 128), BF16),
            pltpu.VMEM((n_head, cols, hidden), BF16),
            pltpu.VMEM((rows, width), BF16),
            pltpu.VMEM((users * cand, width), BF16),
            pltpu.VMEM((rows, cols), BF16),
            pltpu.VMEM((rows, cols), BF16),
            pltpu.VMEM((rows, cols), BF16),
            pltpu.VMEM((rows, cols), F32),
            pltpu.VMEM((rows, cols), F32),
            pltpu.VMEM((24, span), F32),
            pltpu.VMEM((pairs, chunks, DH, DH), F32),
            pltpu.VMEM((pairs, DH, DH), F32),
            pltpu.VMEM((n_ctx, 8, 128), F32),
            pltpu.VMEM((pairs, DH, DH), wire),
            pltpu.VMEM((pairs, DH, DH), wire),
            pltpu.VMEM((pairs, DH, DH), wire),
            pltpu.VMEM((pairs, DH, DH), wire),
            pltpu.VMEM((users, cand, cols), BF16),
            pltpu.VMEM((n_head, users, share, cols), BF16),
            dma((13,)),
            dma((n_ctx,)),
            dma((n_ctx,)),
            dma((pairs,)),
            dma((pairs,)),
            dma((pairs,)),
            dma((pairs,)),
            dma((2 * n_head,)),
            dma((n_head,)),
            dma((users, n_head)),
            dma((users, n_head)),
        ],
        compiler_params=pltpu.CompilerParams(
            collective_id=0, has_side_effects=True, vmem_limit_bytes=60 * 1024 * 1024
        ),
        cost_estimate=pl.CostEstimate(
            flops=flops, bytes_accessed=6 * 1024 * 1024, transcendentals=0
        ),
    )(
        history_len,
        behavior_embed,
        behavior_mask,
        log_decay,
        candidate_embed,
        input_weight,
        input_gain.reshape(1, width),
        proj_weight,
        output_gain.reshape(1, cols),
        ranker_first,
        ranker_second.reshape(hidden // 128, 128),
    )
    return pl.pallas_call(
        results,
        out_shape=(
            jax.ShapeDtypeStruct(history_out.shape, BF16),
            jax.ShapeDtypeStruct(scores.shape, F32),
        ),
        in_specs=[vmem_spec, vmem_spec],
        out_specs=(hbm_spec, hbm_spec),
        scratch_shapes=[dma((users + 1,))],
        compiler_params=pltpu.CompilerParams(vmem_limit_bytes=8 * 1024 * 1024),
        cost_estimate=pl.CostEstimate(flops=0, bytes_accessed=1024 * 1024, transcendentals=0),
    )(history_out, scores)


def solution(mesh):
    in_specs = (
        P("grp", "ctx", None),
        P("grp", "ctx"),
        P("grp"),
        P("head", "grp", "ctx"),
        P("grp", "ctx", None),
        P(),
        P(),
        P(None, None, "head"),
        P("head"),
        P("head", None),
        P(),
    )
    out_specs = (P("grp", "ctx", "head"), P("grp", ("ctx", "head")))
    return jax.shard_map(
        functools.partial(local, mesh.shape["ctx"], mesh.shape["head"]),
        mesh=mesh,
        in_specs=in_specs,
        out_specs=out_specs,
        check_vma=False,
    )
```
